256 devices in a mesh: gx: 8 (over z), gy: 8 (over x, y_lo), gz: 4 (over y_hi, core).
Axes of the slice: x: 4, y: 4 (y_hi: 2, y_lo: 2; y = y_hi * 2 + y_lo), z: 8, core: 2. Of those that a mesh axis runs over, the one named last changes fastest.
Arguments:
- data: float32 [16, 1024, 1024], P('gz', 'gx', 'gy'), may hold values from -6 to 6
- weight: float32 [16, 1024, 1024], P('gz', 'gx', 'gy'), may hold values from 0.2 to 2
- dual_start: float32 [3, 16, 1024, 1024], P(None, 'gz', 'gx', 'gy'), may hold values from -3 to 3
- dual_mid: float32 [3, 16, 1024, 1024], P(None, 'gz', 'gx', 'gy'), may hold values from -3 to 3
- cotangent: float32 [3, 16, 1024, 1024], P(None, 'gz', 'gx', 'gy'), may hold values from -6 to 6
Outputs:
- dual_grad: float32 [3, 16, 1024, 1024], P(None, 'gz', 'gx', 'gy')
- weight_grad: float32 [16, 1024, 1024], P('gz', 'gx', 'gy')
- data_grad: float32 [16, 1024, 1024], P('gz', 'gx', 'gy')
The draws below stay inside these ranges and needn't reach their ends.
All inputs are finite; a program needn't handle non-finite values.
Results may differ from the reference program's by a relative error of at most 0.00002.
Values sent between devices are 32-bit elements; how exact they have to be, the bound alone decides.
A program may use at most 64 MiB of HBM per device.

```python
import math
import jax
import jax.numpy as jnp
from jax import lax

NP = 16
NR = 1024
NC = 1024


def block_scale(stream_key, extent, split, least, largest):
    def one(dim, shards_of):
        heights = jax.random.uniform(jax.random.fold_in(jax.random.fold_in(stream_key, 6), dim), (shards_of,), jnp.float32, least / len(split), largest / len(split))
        return jnp.repeat(jnp.exp(heights), extent[dim] // shards_of).reshape((-1,) + (1,) * (len(extent) - dim - 1))

    loudness = one(*split[0])
    for cut in split[1:]:
        loudness = loudness * one(*cut)
    return loudness


def bell_draw(key, extent, spread, most, pieces=(), held_as=jnp.bfloat16):
    loudness = block_scale(key, extent, pieces, -0.22, 0.18) if pieces else 1.0
    result = jax.random.normal(key, extent, jnp.float32) * spread * loudness
    return jnp.minimum(jnp.maximum(result, -most), most).astype(held_as)


def setup_inputs(seed: int = 0) -> dict:
    keys = jax.random.split(jax.random.key(seed), 6)
    data = bell_draw(keys[0], (NP, NR, NC), 1.0, 6.0, ((0, 4), (1, 8), (2, 8)), jnp.float32)
    weight = jnp.clip(jnp.exp(math.log(2.0) - 2.3025851 * jax.random.uniform(keys[1], (NP, NR, NC), jnp.float32) ** block_scale(keys[1], (NP, NR, NC), ((0, 4), (1, 8), (2, 8)), -0.2, 0.2)), 0.2, 2.0)
    dual_start = bell_draw(keys[2], (3, NP, NR, NC), 0.5, 3.0, ((1, 4), (2, 8), (3, 8)), jnp.float32)
    dual_mid = bell_draw(keys[3], (3, NP, NR, NC), 0.5, 3.0, ((1, 4), (2, 8), (3, 8)), jnp.float32)
    cotangent = bell_draw(keys[4], (3, NP, NR, NC), 1.0, 6.0, ((1, 4), (2, 8), (3, 8)), jnp.float32)
    return dict(data=data, weight=weight, dual_start=dual_start, dual_mid=dual_mid, cotangent=cotangent)


step_size = 0.08
inverse_lambda = 0.5
smoothing = 0.01

def forward_diff(field, axis):
    count = field.shape[axis]
    after = jnp.concatenate([lax.slice_in_dim(field, 1, count, axis=axis), jnp.zeros_like(lax.slice_in_dim(field, 0, 1, axis=axis))], axis)
    return after - field

def backward_diff(field, axis):
    count = field.shape[axis]
    before = jnp.concatenate([jnp.zeros_like(lax.slice_in_dim(field, 0, 1, axis=axis)), lax.slice_in_dim(field, 0, count - 1, axis=axis)], axis)
    return field - before

def divergence(dual):
    total = backward_diff(dual[0], 0)
    total = total + backward_diff(dual[1], 1)
    return total + backward_diff(dual[2], 2)

def gradient(field):
    return jnp.stack([forward_diff(field, 0), forward_diff(field, 1), forward_diff(field, 2)])

def adjoint_step(dual, weight, data, cot):
    values = divergence(dual) - data * inverse_lambda
    slopes = gradient(values)
    norm = jnp.sqrt(lax.optimization_barrier(jnp.sum(slopes * slopes, axis=0)) + smoothing)
    denom = 1.0 + step_size * norm / weight
    update = (dual + step_size * slopes) / denom
    inner = lax.optimization_barrier(jnp.sum(cot * update, axis=0))
    weight_part = inner * step_size * norm / (denom * weight * weight)
    norm_scale = -inner * step_size / (denom * weight)
    slope_cot = step_size * cot / denom + norm_scale / norm * slopes
    value_cot = -divergence(slope_cot)
    dual_cot = cot / denom - gradient(value_cot)
    return (dual_cot, weight_part, -value_cot * inverse_lambda)

def reference(data, weight, dual_start, dual_mid, cotangent):
    cot_mid, weight_mid, data_mid = adjoint_step(dual_mid, weight, data, cotangent)
    cot_start, weight_start, data_start = adjoint_step(dual_start, weight, data, cot_mid)
    return (cot_start, weight_start + weight_mid, data_start + data_mid)
```

```python
import functools

import jax
import jax.numpy as jnp
from jax import lax
from jax.experimental import pallas as pl
from jax.experimental.pallas import tpu as pltpu
from jax.sharding import PartitionSpec as P

MESH = pl.DeviceIdType.MESH
TAU = 0.08
KAPPA = 0.5
DELTA = 0.01
AXES = ("gx", "gy", "gz")

NPL, NRW, NCL = 4, 128, 128
CH = 32
PAD = 8
R, Z, C = 0, 1, 2
SLOTS = (
    ((-1, 0, 0), R),
    ((1, 0, 0), R),
    ((0, -1, 0), C),
    ((0, 1, 0), C),
    ((-1, 0, 1), R),
    ((1, 0, -1), Z),
    ((0, -1, 1), C),
    ((0, 1, -1), Z),
    ((1, -1, 0), C),
    ((-1, 1, 0), R),
    ((0, 0, -1), None),
    ((0, 0, 1), None),
)
NS = len(SLOTS)
F32 = jnp.float32


def exists(pos, sizes, off):
    ok = None
    for p, n, o in zip(pos, sizes, off):
        if o == 0:
            continue
        here = p >= 1 if o < 0 else p < n - 1
        ok = here if ok is None else jnp.logical_and(ok, here)
    return ok


def kernel(
    sizes,
    data_h, weight_h, ps_h, pm_h, cot_h,
    dual_o, wg_o, dg_o,
    data, weight, cot, q_all, u, v_m, v_s, hc, gs, aux, wacc, xbuf, tbuf, tile, rcv, pln,
    in_sem, send_sem, recv_sem,
):
    pos = tuple(lax.axis_index(a) for a in AXES)
    pm, ps, cm, cs = 0, 1, 2, 3
    loads = (
        pltpu.make_async_copy(pm_h, q_all.at[pm, :, 1 : NPL + 1, PAD : PAD + NRW], in_sem.at[0]),
        pltpu.make_async_copy(data_h, data, in_sem.at[1]),
        pltpu.make_async_copy(ps_h, q_all.at[ps, :, 1 : NPL + 1, PAD : PAD + NRW], in_sem.at[2]),
        pltpu.make_async_copy(weight_h, weight, in_sem.at[3]),
        pltpu.make_async_copy(cot_h, cot, in_sem.at[4]),
    )
    for c in loads:
        c.start()

    lane = lax.broadcasted_iota(jnp.int32, (CH, NCL), 1)
    lane8 = lax.broadcasted_iota(jnp.int32, (NPL, NCL), 1)
    sub4 = lax.broadcasted_iota(jnp.int32, (NPL, NCL), 0)

    for s, (off, kind) in enumerate(SLOTS):
        @pl.when(jnp.logical_not(exists(pos, sizes, off)))
        def _():
            for e in range(4):
                if kind is None:
                    pln[e, s - 10] = jnp.zeros((NRW, NCL), F32)
                else:
                    rcv[e, s] = jnp.zeros((8, NCL), F32)

    barrier = pltpu.get_barrier_semaphore()
    for off, _ in SLOTS:
        @pl.when(exists(pos, sizes, off))
        def _():
            peer = tuple(p + o for p, o in zip(pos, off))
            pl.semaphore_signal(barrier, inc=1, device_id=peer, device_id_type=MESH)

    for e in range(4):
        q_all[e, 0, 0, PAD : PAD + NRW] = jnp.zeros((NRW, NCL), F32)
        for k in range(NPL):
            q_all[e, 1, k + 1, 0:PAD] = jnp.zeros((PAD, NCL), F32)

    peers = sum(jnp.where(exists(pos, sizes, off), 1, 0) for off, _ in SLOTS)
    pl.semaphore_wait(barrier, peers)

    def message(e, s):
        off, kind = SLOTS[s]
        if kind is None:
            src = q_all.at[e, 0, NPL, PAD : PAD + NRW] if s == 10 else u.at[e, 0]
            dst = pln.at[e, s - 10]
        else:
            src = tile.at[e, 8 * kind : 8 * kind + 8]
            dst = rcv.at[e, s]
        peer = tuple(p - o for p, o in zip(pos, off))
        return pltpu.make_async_remote_copy(
            src_ref=src, dst_ref=dst, send_sem=send_sem.at[e, s], recv_sem=recv_sem.at[e, s],
            device_id=peer, device_id_type=MESH,
        )

    def send(e, s):
        off = SLOTS[s][0]
        @pl.when(exists(pos, sizes, tuple(-o for o in off)))
        def _():
            message(e, s).start()

    def arrive(e, s):
        @pl.when(exists(pos, sizes, SLOTS[s][0]))
        def _():
            message(e, s).wait_recv()

    def divide_part(e, k, j, extra):
        rows = slice(PAD + CH * j, PAD + CH * (j + 1))
        above = slice(PAD + CH * j - 1, PAD + CH * (j + 1) - 1)
        out = slice(CH * j, CH * (j + 1))
        q2 = q_all[e, 2, k + 1, rows]
        total = q_all[e, 0, k + 1, rows] - q_all[e, 0, k, rows]
        total = total + (q_all[e, 1, k + 1, rows] - q_all[e, 1, k + 1, above])
        total = total + (q2 - jnp.where(lane == 0, 0.0, pltpu.roll(q2, 1, 1)))
        if extra:
            total = total - KAPPA * data[k, out]
        u[e, k, out] = total
        x = jnp.where(lane == k, pltpu.roll(q2, k + 1, 1), xbuf[out])
        xbuf[out] = jnp.where(lane == k + NPL, pltpu.roll(total, k + NPL, 1), x)

    def send_all(e):
        for j in range(NRW // CH):
            rows = slice(PAD + CH * j, PAD + CH * (j + 1))
            out = slice(CH * j, CH * (j + 1))
            xbuf[out] = jnp.where(lane == 8, pltpu.roll(q_all[e, 0, NPL, rows], 8, 1), xbuf[out])
        send(e, 10)
        send(e, 11)
        xt = jnp.transpose(xbuf[...])
        tile[e, 16:24] = xt[0:8]
        tile[e, 9:10] = xt[8:9]
        tile[e, 8:9] = q_all[e, 0, NPL, PAD : PAD + 1]
        for k in range(NPL):
            tile[e, k : k + 1] = q_all[e, 1, k + 1, PAD + NRW - 1 : PAD + NRW]
            tile[e, k + NPL : k + NPL + 1] = u[e, k, 0:1]
        for s in range(10):
            send(e, s)

    def receive(e, v):
        for s in range(NS):
            arrive(e, s)
        up_x = exists(pos, sizes, (1, 0, 0))
        up_y = exists(pos, sizes, (0, 1, 0))
        up_z = exists(pos, sizes, (0, 0, 1))
        low_c = rcv[e, 2, 0:NPL]
        high_c = rcv[e, 3, NPL : 2 * NPL] - tile[e, 16 : 16 + NPL]
        high_c = high_c - jnp.where(sub4 == 0, rcv[e, 7, 1:2], 0.0)
        high_c = high_c - jnp.where(lane8 == 0, rcv[e, 9, 0:NPL], 0.0)
        high_c = jnp.where(up_y, high_c, 0.0)
        tbuf[0:NPL] = low_c
        tbuf[NPL : 2 * NPL] = high_c
        tbuf[8:16] = rcv[e, 6]
        tbuf[...] = jnp.transpose(tbuf[...])

        def planes(k, _):
            for j in range(NRW // CH):
                out = slice(CH * j, CH * (j + 1))
                col = pltpu.roll(tbuf[out], NCL - k, 1)
                v[k, out] = u[e, k, out] - jnp.where(lane == 0, col, 0.0)
            return 0

        lax.fori_loop(0, NPL, planes, 0)
        high_r = rcv[e, 1, NPL : 2 * NPL] - tile[e, 0:NPL]
        high_r = high_r - jnp.where(sub4 == 0, rcv[e, 5, 0:1], 0.0)
        high_r = high_r - jnp.where(lane8 == 0, rcv[e, 8, 0:NPL], 0.0)
        high_r = jnp.where(up_x, high_r, 0.0)
        for k in range(NPL):
            v[k, 0:1] = v[k, 0:1] - rcv[e, 0, k : k + 1]
            v[k, NRW : NRW + 1] = high_r[k : k + 1]
        for j in range(NRW // CH):
            rows = slice(PAD + CH * j, PAD + CH * (j + 1))
            out = slice(CH * j, CH * (j + 1))
            v[0, out] = v[0, out] - pln[e, 0, out]
            col = jnp.where(lane == 0, pltpu.roll(tbuf[out], NCL - 8, 1), 0.0)
            v[NPL, out] = jnp.where(up_z, pln[e, 1, out] - q_all[e, 0, NPL, rows] - col, 0.0)
        v[NPL, 0:1] = v[NPL, 0:1] - jnp.where(up_z, rcv[e, 4, 0:1], 0.0)

    def slopes(v, k, j):
        out = slice(CH * j, CH * (j + 1))
        c = v[k, out]
        col = pltpu.roll(tbuf[out], NCL - 1 - NPL - k, 1)
        return (
            v[k + 1, out] - c,
            v[k, CH * j + 1 : CH * (j + 1) + 1] - c,
            jnp.where(lane == NCL - 1, col, pltpu.roll(c, NCL - 1, 1)) - c,
        )

    def each_chunk(body):
        def planes(k, _):
            for j in range(NRW // CH):
                body(k, j)
            return 0
        lax.fori_loop(0, NPL, planes, 0)

    def spots(j):
        return slice(PAD + CH * j, PAD + CH * (j + 1)), slice(CH * j, CH * (j + 1))

    loads[0].wait()
    loads[1].wait()
    each_chunk(lambda k, j: divide_part(pm, k, j, True))
    send_all(pm)
    loads[2].wait()
    each_chunk(lambda k, j: divide_part(ps, k, j, True))
    send_all(ps)
    loads[3].wait()
    loads[4].wait()

    receive(pm, v_m)

    def adjoint_mid(k, j):
        rows, out = spots(j)
        g = slopes(v_m, k, j)
        t = g[0] * g[0] + g[1] * g[1] + g[2] * g[2] + DELTA
        rn = lax.rsqrt(t)
        n = t * rn
        w = weight[k, out]
        r = 1.0 / (w + TAU * n)
        h = w * r
        c = [cot[a, k, out] for a in range(3)]
        s = None
        for a in range(3):
            term = c[a] * (q_all[pm, a, k + 1, rows] + TAU * g[a])
            s = term if s is None else s + term
        m = TAU * r * (h * s)
        wacc[k, out] = m * n
        f = m * rn
        for a in range(3):
            hc_a = h * c[a]
            hc[a, k, out] = hc_a
            q_all[cm, a, k + 1, rows] = TAU * hc_a - f * g[a]
        divide_part(cm, k, j, False)

    each_chunk(adjoint_mid)
    send_all(cm)

    receive(ps, v_s)

    def prepare_start(k, j):
        rows, out = spots(j)
        g = slopes(v_s, k, j)
        t = g[0] * g[0] + g[1] * g[1] + g[2] * g[2] + DELTA
        rn = lax.rsqrt(t)
        n = t * rn
        w = weight[k, out]
        r = 1.0 / (w + TAU * n)
        h = w * r
        a1 = TAU * r * h
        aux[0, k, out] = h
        aux[1, k, out] = a1 * rn
        aux[2, k, out] = a1 * n
        for a in range(3):
            gs[a, k, out] = g[a]

    each_chunk(prepare_start)

    receive(cm, v_m)

    def adjoint_start(k, j):
        rows, out = spots(j)
        d = slopes(v_m, k, j)
        h = aux[0, k, out]
        g = [gs[a, k, out] for a in range(3)]
        c = [hc[a, k, out] + d[a] for a in range(3)]
        s = None
        for a in range(3):
            term = c[a] * (q_all[ps, a, k + 1, rows] + TAU * g[a])
            s = term if s is None else s + term
        wacc[k, out] = wacc[k, out] + aux[2, k, out] * s
        f = aux[1, k, out] * s
        for a in range(3):
            hc_a = h * c[a]
            hc[a, k, out] = hc_a
            q_all[cs, a, k + 1, rows] = TAU * hc_a - f * g[a]
        divide_part(cs, k, j, False)

    each_chunk(adjoint_start)
    send_all(cs)

    def finish_weight(k, j):
        _, out = spots(j)
        wg_o[k, out] = wacc[k, out] / weight[k, out]

    each_chunk(finish_weight)
    receive(cs, v_s)

    def finish(k, j):
        _, out = spots(j)
        d = slopes(v_s, k, j)
        for a in range(3):
            dual_o[a, k, out] = hc[a, k, out] + d[a]
        dg_o[k, out] = KAPPA * (v_s[k, out] + v_m[k, out])

    each_chunk(finish)
    for e in range(4):
        for s in range(NS):
            off = SLOTS[s][0]
            @pl.when(exists(pos, sizes, tuple(-o for o in off)))
            def _():
                message(e, s).wait_send()


def shards(sizes, data, weight, dual_start, dual_mid, cotangent):
    field = (NPL, NRW, NCL)
    vm = pltpu.VMEM
    whole = pl.BlockSpec(memory_space=pltpu.VMEM)
    return pl.pallas_call(
        functools.partial(kernel, sizes),
        out_shape=(
            jax.ShapeDtypeStruct((3,) + field, F32),
            jax.ShapeDtypeStruct(field, F32),
            jax.ShapeDtypeStruct(field, F32),
        ),
        in_specs=[pl.BlockSpec(memory_space=pl.ANY)] * 5,
        out_specs=(whole,) * 3,
        scratch_shapes=[
            vm(field, F32),
            vm(field, F32),
            vm((3,) + field, F32),
            vm((4, 3, NPL + 1, NRW + PAD, NCL), F32),
            vm((4,) + field, F32),
            vm((NPL + 1, NRW + PAD, NCL), F32),
            vm((NPL + 1, NRW + PAD, NCL), F32),
            vm((3,) + field, F32),
            vm((3,) + field, F32),
            vm((3,) + field, F32),
            vm(field, F32),
            vm((NRW, NCL), F32),
            vm((NRW, NCL), F32),
            vm((4, 24, NCL), F32),
            vm((4, 10, 8, NCL), F32),
            vm((4, 2, NRW, NCL), F32),
            pltpu.SemaphoreType.DMA((5,)),
            pltpu.SemaphoreType.DMA((4, NS)),
            pltpu.SemaphoreType.DMA((4, NS)),
        ],
        compiler_params=pltpu.CompilerParams(
            collective_id=0, has_side_effects=True, vmem_limit_bytes=40 * 1024 * 1024
        ),
    )(data, weight, dual_start, dual_mid, cotangent)


def solution(mesh):
    field, triple = P("gz", "gx", "gy"), P(None, "gz", "gx", "gy")
    sizes = tuple(mesh.shape[a] for a in AXES)
    return jax.shard_map(
        functools.partial(shards, sizes),
        mesh=mesh,
        in_specs=(field, field, triple, triple, triple),
        out_specs=(triple, field, field),
        check_vma=False,
    )
```

```python
import functools

import jax
import jax.numpy as jnp
from jax import lax
from jax.experimental import pallas as pl
from jax.experimental.pallas import tpu as pltpu
from jax.sharding import PartitionSpec as P

MESH = pl.DeviceIdType.MESH
TAU = 0.08
KAPPA = 0.5
DELTA = 0.01
AXES = ("gx", "gy", "gz")

NPL, NRW, NCL = 4, 128, 128
CH = 32
PAD = 8
R, Z, C = 0, 1, 2
SLOTS = (
    ((-1, 0, 0), R),
    ((1, 0, 0), R),
    ((0, -1, 0), C),
    ((0, 1, 0), C),
    ((-1, 0, 1), R),
    ((1, 0, -1), Z),
    ((0, -1, 1), C),
    ((0, 1, -1), Z),
    ((1, -1, 0), C),
    ((-1, 1, 0), R),
    ((0, 0, -1), None),
    ((0, 0, 1), None),
)
NS = len(SLOTS)
F32 = jnp.float32


def kernel(
    sizes,
    data_h, weight_h, ps_h, pm_h, cot_h,
    dual_o, wg_o, dg_o,
    data, weight, cot, q_all, u, v_m, v_s, hc, gs, aux, wacc, xbuf, tbuf, tile, rcv, pln, spare,
    in_sem, send_sem, recv_sem,
):
    pos = tuple(lax.axis_index(a) for a in AXES)
    pm, ps, cm, cs = 0, 1, 2, 3
    loads = (
        pltpu.make_async_copy(pm_h, q_all.at[pm, :, 1 : NPL + 1, PAD : PAD + NRW], in_sem.at[0]),
        pltpu.make_async_copy(data_h, data, in_sem.at[1]),
        pltpu.make_async_copy(ps_h, q_all.at[ps, :, 1 : NPL + 1, PAD : PAD + NRW], in_sem.at[2]),
        pltpu.make_async_copy(weight_h, weight, in_sem.at[3]),
        pltpu.make_async_copy(cot_h, cot, in_sem.at[4]),
    )
    for c in loads:
        c.start()

    lane = lax.broadcasted_iota(jnp.int32, (CH, NCL), 1)
    lane8 = lax.broadcasted_iota(jnp.int32, (NPL, NCL), 1)
    sub4 = lax.broadcasted_iota(jnp.int32, (NPL, NCL), 0)

    low_x, low_y, low_z = (p > 0 for p in pos)
    up_x, up_y, up_z = (p < n - 1 for p, n in zip(pos, sizes))

    def exists(off):
        ok = None
        for o, low, up in zip(off, (low_x, low_y, low_z), (up_x, up_y, up_z)):
            if o != 0:
                here = low if o < 0 else up
                ok = here if ok is None else jnp.logical_and(ok, here)
        return ok

    has = [exists(off) for off, _ in SLOTS]
    takes = [exists(tuple(-o for o in off)) for off, _ in SLOTS]
    barrier = pltpu.get_barrier_semaphore()
    for (off, _), here in zip(SLOTS, has):
        @pl.when(here)
        def _():
            peer = tuple(p + o for p, o in zip(pos, off))
            pl.semaphore_signal(barrier, inc=1, device_id=peer, device_id_type=MESH)

    for side, here in ((0, low_z), (1, up_z)):
        @pl.when(jnp.logical_not(here))
        def _():
            for e in range(4):
                pln[e, side] = jnp.zeros((NRW, NCL), F32)

    for e in range(4):
        q_all[e, 0, 0, PAD : PAD + NRW] = jnp.zeros((NRW, NCL), F32)
        for k in range(NPL):
            q_all[e, 1, k + 1, 0:PAD] = jnp.zeros((PAD, NCL), F32)

    pl.semaphore_wait(barrier, sum(jnp.where(here, 1, 0) for here in has))

    def message(e, s):
        off, kind = SLOTS[s]
        if kind is None:
            src = q_all.at[e, 0, NPL, PAD : PAD + NRW] if s == 10 else u.at[e, 0]
            dst, sem = pln.at[e, s - 10], s - 9
        else:
            src, dst, sem = tile.at[e, 8 * kind : 8 * kind + 8], rcv.at[e, s], 0
        return pltpu.make_async_remote_copy(
            src_ref=src, dst_ref=dst, send_sem=send_sem.at[e, sem], recv_sem=recv_sem.at[e, sem],
            device_id=tuple(p - o for p, o in zip(pos, off)), device_id_type=MESH,
        )

    def filler(e, s, sem):
        kind = SLOTS[s][1]
        dst = rcv.at[e, s] if sem is recv_sem else spare.at[e, s]
        return pltpu.make_async_copy(tile.at[e, 8 * kind : 8 * kind + 8], dst, sem.at[e, 0])

    def tiles_done(e, sem):
        pltpu.make_async_copy(rcv.at[e], rcv.at[e], sem.at[e, 0]).wait()

    def divide_part(e, k, j, extra):
        rows = slice(PAD + CH * j, PAD + CH * (j + 1))
        above = slice(PAD + CH * j - 1, PAD + CH * (j + 1) - 1)
        out = slice(CH * j, CH * (j + 1))
        q2 = q_all[e, 2, k + 1, rows]
        total = q_all[e, 0, k + 1, rows] - q_all[e, 0, k, rows]
        total = total + (q_all[e, 1, k + 1, rows] - q_all[e, 1, k + 1, above])
        total = total + (q2 - jnp.where(lane == 0, 0.0, pltpu.roll(q2, 1, 1)))
        if extra:
            total = total - KAPPA * data[k, out]
        u[e, k, out] = total
        x = jnp.where(lane == k, pltpu.roll(q2, k + 1, 1), xbuf[out])
        xbuf[out] = jnp.where(lane == k + NPL, pltpu.roll(total, k + NPL, 1), x)

    def send_all(e):
        for j in range(NRW // CH):
            rows = slice(PAD + CH * j, PAD + CH * (j + 1))
            out = slice(CH * j, CH * (j + 1))
            xbuf[out] = jnp.where(lane == 8, pltpu.roll(q_all[e, 0, NPL, rows], 8, 1), xbuf[out])
        pl.when(up_z)(lambda: message(e, 10).start())
        pl.when(low_z)(lambda: message(e, 11).start())
        xt = jnp.transpose(xbuf[...])
        tile[e, 16:24] = xt[0:8]
        tile[e, 9:10] = xt[8:9]
        tile[e, 8:9] = q_all[e, 0, NPL, PAD : PAD + 1]
        for k in range(NPL):
            tile[e, k : k + 1] = q_all[e, 1, k + 1, PAD + NRW - 1 : PAD + NRW]
            tile[e, k + NPL : k + NPL + 1] = u[e, k, 0:1]
        for s in range(10):
            pl.when(takes[s])(lambda: message(e, s).start())
            pl.when(jnp.logical_not(takes[s]))(lambda: filler(e, s, send_sem).start())
            pl.when(jnp.logical_not(has[s]))(lambda: filler(e, s, recv_sem).start())

    def receive(e, v):
        tiles_done(e, recv_sem)
        low_c = jnp.where(low_y, rcv[e, 2, 0:NPL], 0.0)
        high_c = rcv[e, 3, NPL : 2 * NPL] - tile[e, 16 : 16 + NPL]
        high_c = high_c - jnp.where(jnp.logical_and(sub4 == 0, low_z), rcv[e, 7, 1:2], 0.0)
        high_c = high_c - jnp.where(jnp.logical_and(lane8 == 0, low_x), rcv[e, 9, 0:NPL], 0.0)
        high_c = jnp.where(up_y, high_c, 0.0)
        tbuf[0:NPL] = low_c
        tbuf[NPL : 2 * NPL] = high_c
        tbuf[8:16] = jnp.where(low_y, rcv[e, 6], 0.0)
        tbuf[...] = jnp.transpose(tbuf[...])

        def planes(k, _):
            for j in range(NRW // CH):
                out = slice(CH * j, CH * (j + 1))
                col = pltpu.roll(tbuf[out], NCL - k, 1)
                v[k, out] = u[e, k, out] - jnp.where(lane == 0, col, 0.0)
            return 0

        lax.fori_loop(0, NPL, planes, 0)
        high_r = rcv[e, 1, NPL : 2 * NPL] - tile[e, 0:NPL]
        high_r = high_r - jnp.where(jnp.logical_and(sub4 == 0, low_z), rcv[e, 5, 0:1], 0.0)
        high_r = high_r - jnp.where(jnp.logical_and(lane8 == 0, low_y), rcv[e, 8, 0:NPL], 0.0)
        high_r = jnp.where(up_x, high_r, 0.0)
        low_r = jnp.where(low_x, rcv[e, 0, 0:NPL], 0.0)
        for k in range(NPL):
            v[k, 0:1] = v[k, 0:1] - low_r[k : k + 1]
            v[k, NRW : NRW + 1] = high_r[k : k + 1]
        pl.when(low_z)(lambda: message(e, 10).wait_recv())
        pl.when(up_z)(lambda: message(e, 11).wait_recv())
        for j in range(NRW // CH):
            rows = slice(PAD + CH * j, PAD + CH * (j + 1))
            out = slice(CH * j, CH * (j + 1))
            v[0, out] = v[0, out] - pln[e, 0, out]
            col = jnp.where(lane == 0, pltpu.roll(tbuf[out], NCL - 8, 1), 0.0)
            v[NPL, out] = jnp.where(up_z, pln[e, 1, out] - q_all[e, 0, NPL, rows] - col, 0.0)
        v[NPL, 0:1] = v[NPL, 0:1] - jnp.where(jnp.logical_and(up_z, low_x), rcv[e, 4, 0:1], 0.0)

    def slopes(v, k, j):
        out = slice(CH * j, CH * (j + 1))
        c = v[k, out]
        col = pltpu.roll(tbuf[out], NCL - 1 - NPL - k, 1)
        return (
            v[k + 1, out] - c,
            v[k, CH * j + 1 : CH * (j + 1) + 1] - c,
            jnp.where(lane == NCL - 1, col, pltpu.roll(c, NCL - 1, 1)) - c,
        )

    def each_chunk(body):
        def planes(k, _):
            for j in range(NRW // CH):
                body(k, j)
            return 0
        lax.fori_loop(0, NPL, planes, 0)

    def spots(j):
        return slice(PAD + CH * j, PAD + CH * (j + 1)), slice(CH * j, CH * (j + 1))

    loads[0].wait()
    loads[1].wait()
    each_chunk(lambda k, j: divide_part(pm, k, j, True))
    send_all(pm)
    loads[2].wait()
    each_chunk(lambda k, j: divide_part(ps, k, j, True))
    send_all(ps)
    loads[3].wait()
    loads[4].wait()

    receive(pm, v_m)

    def adjoint_mid(k, j):
        rows, out = spots(j)
        g = slopes(v_m, k, j)
        t = g[0] * g[0] + g[1] * g[1] + g[2] * g[2] + DELTA
        rn = lax.rsqrt(t)
        n = t * rn
        w = weight[k, out]
        r = 1.0 / (w + TAU * n)
        h = w * r
        c = [cot[a, k, out] for a in range(3)]
        s = None
        for a in range(3):
            term = c[a] * (q_all[pm, a, k + 1, rows] + TAU * g[a])
            s = term if s is None else s + term
        m = TAU * r * (h * s)
        wacc[k, out] = m * n
        f = m * rn
        for a in range(3):
            hc_a = h * c[a]
            hc[a, k, out] = hc_a
            q_all[cm, a, k + 1, rows] = TAU * hc_a - f * g[a]
        divide_part(cm, k, j, False)

    each_chunk(adjoint_mid)
    send_all(cm)

    receive(ps, v_s)

    def prepare_start(k, j):
        rows, out = spots(j)
        g = slopes(v_s, k, j)
        t = g[0] * g[0] + g[1] * g[1] + g[2] * g[2] + DELTA
        rn = lax.rsqrt(t)
        n = t * rn
        w = weight[k, out]
        r = 1.0 / (w + TAU * n)
        h = w * r
        a1 = TAU * r * h
        aux[0, k, out] = h
        aux[1, k, out] = a1 * rn
        aux[2, k, out] = a1 * n
        for a in range(3):
            gs[a, k, out] = g[a]

    each_chunk(prepare_start)

    receive(cm, v_m)

    def adjoint_start(k, j):
        rows, out = spots(j)
        d = slopes(v_m, k, j)
        h = aux[0, k, out]
        g = [gs[a, k, out] for a in range(3)]
        c = [hc[a, k, out] + d[a] for a in range(3)]
        s = None
        for a in range(3):
            term = c[a] * (q_all[ps, a, k + 1, rows] + TAU * g[a])
            s = term if s is None else s + term
        wacc[k, out] = wacc[k, out] + aux[2, k, out] * s
        f = aux[1, k, out] * s
        for a in range(3):
            hc_a = h * c[a]
            hc[a, k, out] = hc_a
            q_all[cs, a, k + 1, rows] = TAU * hc_a - f * g[a]
        divide_part(cs, k, j, False)

    each_chunk(adjoint_start)
    send_all(cs)

    def finish_weight(k, j):
        _, out = spots(j)
        wg_o[k, out] = wacc[k, out] / weight[k, out]

    each_chunk(finish_weight)
    receive(cs, v_s)

    def finish(k, j):
        _, out = spots(j)
        d = slopes(v_s, k, j)
        for a in range(3):
            dual_o[a, k, out] = hc[a, k, out] + d[a]
        dg_o[k, out] = KAPPA * (v_s[k, out] + v_m[k, out])

    each_chunk(finish)
    for e in range(4):
        tiles_done(e, send_sem)
        pl.when(up_z)(lambda: message(e, 10).wait_send())
        pl.when(low_z)(lambda: message(e, 11).wait_send())


def write_out(*refs):
    sem = refs[-1]
    copies = [pltpu.make_async_copy(refs[i], refs[i + 3], sem.at[i]) for i in range(3)]
    for c in copies:
        c.start()
    for c in copies:
        c.wait()


def shards(sizes, data, weight, dual_start, dual_mid, cotangent):
    field = (NPL, NRW, NCL)
    vm = pltpu.VMEM
    whole = pl.BlockSpec(memory_space=pltpu.VMEM)
    shapes = (
        jax.ShapeDtypeStruct((3,) + field, F32),
        jax.ShapeDtypeStruct(field, F32),
        jax.ShapeDtypeStruct(field, F32),
    )
    args = (data, weight, dual_start, dual_mid, cotangent)
    results = pl.pallas_call(
        functools.partial(kernel, sizes),
        out_shape=shapes,
        in_specs=[pl.BlockSpec(memory_space=pl.ANY)] * 5,
        out_specs=(whole,) * 3,
        scratch_shapes=[
            vm(field, F32),
            vm(field, F32),
            vm((3,) + field, F32),
            vm((4, 3, NPL + 1, NRW + PAD, NCL), F32),
            vm((4,) + field, F32),
            vm((NPL + 1, NRW + PAD, NCL), F32),
            vm((NPL + 1, NRW + PAD, NCL), F32),
            vm((3,) + field, F32),
            vm((3,) + field, F32),
            vm((3,) + field, F32),
            vm(field, F32),
            vm((NRW, NCL), F32),
            vm((NRW, NCL), F32),
            vm((4, 24, NCL), F32),
            vm((4, 10, 8, NCL), F32),
            vm((4, 2, NRW, NCL), F32),
            vm((4, 10, 8, NCL), F32),
            pltpu.SemaphoreType.DMA((5,)),
            pltpu.SemaphoreType.DMA((4, 3)),
            pltpu.SemaphoreType.DMA((4, 3)),
        ],
        compiler_params=pltpu.CompilerParams(
            collective_id=0, has_side_effects=True, vmem_limit_bytes=40 * 1024 * 1024
        ),
    )(*[pltpu.with_memory_space_constraint(x, pltpu.HBM) for x in args])
    return pl.pallas_call(
        write_out,
        out_shape=shapes,
        in_specs=[pl.BlockSpec(memory_space=pltpu.VMEM)] * 3,
        out_specs=(pl.BlockSpec(memory_space=pl.ANY),) * 3,
        scratch_shapes=[pltpu.SemaphoreType.DMA((3,))],
    )(*[pltpu.with_memory_space_constraint(x, pltpu.VMEM) for x in results])


def solution(mesh):
    field, triple = P("gz", "gx", "gy"), P(None, "gz", "gx", "gy")
    sizes = tuple(mesh.shape[a] for a in AXES)
    return jax.shard_map(
        functools.partial(shards, sizes),
        mesh=mesh,
        in_specs=(field, field, triple, triple, triple),
        out_specs=(triple, field, field),
        check_vma=False,
    )
```

```python
import functools

import jax
import jax.numpy as jnp
from jax import lax
from jax.experimental import pallas as pl
from jax.experimental.pallas import tpu as pltpu
from jax.sharding import PartitionSpec as P

MESH = pl.DeviceIdType.MESH
TAU = 0.08
KAPPA = 0.5
DELTA = 0.01
AXES = ("gx", "gy", "gz")

NPL, NRW, NCL = 4, 128, 128
CH = 32
PAD = 8
R, Z, C = 0, 1, 2
SLOTS = (
    ((-1, 0, 0), R),
    ((1, 0, 0), R),
    ((0, -1, 0), C),
    ((0, 1, 0), C),
    ((-1, 0, 1), R),
    ((1, 0, -1), Z),
    ((0, -1, 1), C),
    ((0, 1, -1), Z),
    ((1, -1, 0), C),
    ((-1, 1, 0), R),
    ((0, 0, -1), None),
    ((0, 0, 1), None),
)
NS = len(SLOTS)
F32 = jnp.float32


def kernel(
    sizes,
    data_h, weight_h, ps_h, pm_h, cot_h,
    dual_o, wg_o, dg_o,
    data, weight, cot, q_all, u, v_m, v_s, hc, gs, aux, wacc, xbuf, tbuf, rbuf, tile, rcv, pln, spare,
    in_sem, send_sem, recv_sem,
):
    pos = tuple(lax.axis_index(a) for a in AXES)
    pm, ps, cm, cs = 0, 1, 2, 3
    rest = slice(1, NPL)
    loads = (
        pltpu.make_async_copy(pm_h.at[:, 0], q_all.at[pm, :, 1, PAD : PAD + NRW], in_sem.at[0]),
        pltpu.make_async_copy(data_h.at[0], data.at[0], in_sem.at[1]),
        pltpu.make_async_copy(pm_h.at[:, rest], q_all.at[pm, :, 2 : NPL + 1, PAD : PAD + NRW], in_sem.at[2]),
        pltpu.make_async_copy(data_h.at[rest], data.at[rest], in_sem.at[3]),
        pltpu.make_async_copy(ps_h, q_all.at[ps, :, 1 : NPL + 1, PAD : PAD + NRW], in_sem.at[4]),
        pltpu.make_async_copy(weight_h, weight, in_sem.at[5]),
        pltpu.make_async_copy(cot_h, cot, in_sem.at[6]),
    )
    for c in loads:
        c.start()

    lane = lax.broadcasted_iota(jnp.int32, (CH, NCL), 1)
    lane8 = lax.broadcasted_iota(jnp.int32, (NPL, NCL), 1)
    sub4 = lax.broadcasted_iota(jnp.int32, (NPL, NCL), 0)

    low_x, low_y, low_z = (p > 0 for p in pos)
    up_x, up_y, up_z = (p < n - 1 for p, n in zip(pos, sizes))

    def exists(off):
        ok = None
        for o, low, up in zip(off, (low_x, low_y, low_z), (up_x, up_y, up_z)):
            if o != 0:
                here = low if o < 0 else up
                ok = here if ok is None else jnp.logical_and(ok, here)
        return ok

    has = [exists(off) for off, _ in SLOTS]
    takes = [exists(tuple(-o for o in off)) for off, _ in SLOTS]
    barrier = pltpu.get_barrier_semaphore()
    for (off, _), here in zip(SLOTS, has):
        @pl.when(here)
        def _():
            peer = tuple(p + o for p, o in zip(pos, off))
            pl.semaphore_signal(barrier, inc=1, device_id=peer, device_id_type=MESH)

    for side, here in ((0, low_z), (1, up_z)):
        @pl.when(jnp.logical_not(here))
        def _():
            for e in range(4):
                pln[e, side] = jnp.zeros((NRW, NCL), F32)

    for e in range(4):
        q_all[e, 0, 0, PAD : PAD + NRW] = jnp.zeros((NRW, NCL), F32)
        for k in range(NPL):
            q_all[e, 1, k + 1, 0:PAD] = jnp.zeros((PAD, NCL), F32)

    pl.semaphore_wait(barrier, sum(jnp.where(here, 1, 0) for here in has))

    def message(e, s):
        off, kind = SLOTS[s]
        if kind is None:
            first = (pm_h.at[0, NPL - 1], ps_h.at[0, NPL - 1], q_all.at[cm, 0, NPL, PAD : PAD + NRW],
                     q_all.at[cs, 0, NPL, PAD : PAD + NRW])
            src = first[e] if s == 10 else u.at[e, 0]
            dst, sem = pln.at[e, s - 10], s - 9
        else:
            src, dst, sem = tile.at[e, 8 * kind : 8 * kind + 8], rcv.at[e, s], 0
        return pltpu.make_async_remote_copy(
            src_ref=src, dst_ref=dst, send_sem=send_sem.at[e, sem], recv_sem=recv_sem.at[e, sem],
            device_id=tuple(p - o for p, o in zip(pos, off)), device_id_type=MESH,
        )

    def filler(e, s, sem):
        kind = SLOTS[s][1]
        dst = rcv.at[e, s] if sem is recv_sem else spare.at[e, s]
        return pltpu.make_async_copy(tile.at[e, 8 * kind : 8 * kind + 8], dst, sem.at[e, 0])

    def tiles_done(e, sem):
        pltpu.make_async_copy(rcv.at[e], rcv.at[e], sem.at[e, 0]).wait()

    def divide_part(e, k, j, extra):
        rows = slice(PAD + CH * j, PAD + CH * (j + 1))
        above = slice(PAD + CH * j - 1, PAD + CH * (j + 1) - 1)
        out = slice(CH * j, CH * (j + 1))
        q2 = q_all[e, 2, k + 1, rows]
        total = q_all[e, 0, k + 1, rows] - q_all[e, 0, k, rows]
        total = total + (q_all[e, 1, k + 1, rows] - q_all[e, 1, k + 1, above])
        total = total + (q2 - jnp.where(lane == 0, 0.0, pltpu.roll(q2, 1, 1)))
        if extra:
            total = total - KAPPA * data[k, out]
        u[e, k, out] = total
        x = jnp.where(lane == k, pltpu.roll(q2, k + 1, 1), xbuf[out])
        xbuf[out] = jnp.where(lane == k + NPL, pltpu.roll(total, k + NPL, 1), x)

    def send_last_plane(e):
        pl.when(up_z)(lambda: message(e, 10).start())

    def send_first_plane(e):
        pl.when(low_z)(lambda: message(e, 11).start())

    def send_tiles(e):
        for j in range(NRW // CH):
            rows = slice(PAD + CH * j, PAD + CH * (j + 1))
            out = slice(CH * j, CH * (j + 1))
            xbuf[out] = jnp.where(lane == 8, pltpu.roll(q_all[e, 0, NPL, rows], 8, 1), xbuf[out])
        xt = jnp.transpose(xbuf[...])
        tile[e, 16:24] = xt[0:8]
        tile[e, 9:10] = xt[8:9]
        tile[e, 8:9] = q_all[e, 0, NPL, PAD : PAD + 1]
        for k in range(NPL):
            tile[e, k : k + 1] = q_all[e, 1, k + 1, PAD + NRW - 1 : PAD + NRW]
            tile[e, k + NPL : k + NPL + 1] = u[e, k, 0:1]
        for s in (6, 7, 8, 9, 2, 3, 4, 5, 0, 1):
            pl.when(takes[s])(lambda: message(e, s).start())
            pl.when(jnp.logical_not(takes[s]))(lambda: filler(e, s, send_sem).start())
            pl.when(jnp.logical_not(has[s]))(lambda: filler(e, s, recv_sem).start())

    def receive_tiles(e):
        tiles_done(e, recv_sem)
        low_c = jnp.where(low_y, rcv[e, 2, 0:NPL], 0.0)
        high_c = rcv[e, 3, NPL : 2 * NPL] - tile[e, 16 : 16 + NPL]
        high_c = high_c - jnp.where(jnp.logical_and(sub4 == 0, low_z), rcv[e, 7, 1:2], 0.0)
        high_c = high_c - jnp.where(jnp.logical_and(lane8 == 0, low_x), rcv[e, 9, 0:NPL], 0.0)
        tbuf[0:NPL] = low_c
        tbuf[NPL : 2 * NPL] = jnp.where(up_y, high_c, 0.0)
        tbuf[8:16] = jnp.where(low_y, rcv[e, 6], 0.0)
        tbuf[...] = jnp.transpose(tbuf[...])
        high_r = rcv[e, 1, NPL : 2 * NPL] - tile[e, 0:NPL]
        high_r = high_r - jnp.where(jnp.logical_and(sub4 == 0, low_z), rcv[e, 5, 0:1], 0.0)
        high_r = high_r - jnp.where(jnp.logical_and(lane8 == 0, low_y), rcv[e, 8, 0:NPL], 0.0)
        rbuf[0:NPL] = jnp.where(low_x, rcv[e, 0, 0:NPL], 0.0)
        rbuf[NPL : 2 * NPL] = jnp.where(up_x, high_r, 0.0)

    def fix(e, v, k):
        if k == 0:
            pl.when(low_z)(lambda: message(e, 10).wait_recv())
        for j in range(NRW // CH):
            out = slice(CH * j, CH * (j + 1))
            total = u[e, k, out] - jnp.where(lane == 0, pltpu.roll(tbuf[out], (NCL - k) % NCL, 1), 0.0)
            if k == 0:
                total = total - pln[e, 0, out]
            v[k, out] = total
        v[k, 0:1] = v[k, 0:1] - rbuf[k : k + 1]
        v[k, NRW : NRW + 1] = rbuf[NPL + k : NPL + k + 1]

    def fix_beyond(e, v):
        pl.when(up_z)(lambda: message(e, 11).wait_recv())
        for j in range(NRW // CH):
            rows = slice(PAD + CH * j, PAD + CH * (j + 1))
            out = slice(CH * j, CH * (j + 1))
            col = jnp.where(lane == 0, pltpu.roll(tbuf[out], NCL - 8, 1), 0.0)
            v[NPL, out] = jnp.where(up_z, pln[e, 1, out] - q_all[e, 0, NPL, rows] - col, 0.0)
        v[NPL, 0:1] = v[NPL, 0:1] - jnp.where(jnp.logical_and(up_z, low_x), rcv[e, 4, 0:1], 0.0)

    def slopes(v, k, j):
        out = slice(CH * j, CH * (j + 1))
        c = v[k, out]
        col = pltpu.roll(tbuf[out], NCL - 1 - NPL - k, 1)
        return (
            v[k + 1, out] - c,
            v[k, CH * j + 1 : CH * (j + 1) + 1] - c,
            jnp.where(lane == NCL - 1, col, pltpu.roll(c, NCL - 1, 1)) - c,
        )

    def plane(body, k):
        for j in range(NRW // CH):
            body(k, j)

    def parts(e, k, extra=False):
        plane(lambda k, j: divide_part(e, k, j, extra), k)

    def spots(j):
        return slice(PAD + CH * j, PAD + CH * (j + 1)), slice(CH * j, CH * (j + 1))

    def step(e, v, body, nxt):
        receive_tiles(e)
        fix(e, v, 3)
        fix_beyond(e, v)
        plane(body, 3)
        send_last_plane(nxt)
        fix(e, v, 0)
        fix(e, v, 1)
        plane(body, 0)
        parts(nxt, 0)
        send_first_plane(nxt)
        fix(e, v, 2)
        for k in (1, 2):
            plane(body, k)
            parts(nxt, k)
        parts(nxt, 3)
        send_tiles(nxt)

    send_last_plane(pm)
    loads[0].wait()
    loads[1].wait()
    parts(pm, 0, True)
    send_first_plane(pm)
    loads[2].wait()
    loads[3].wait()
    for k in range(1, NPL):
        parts(pm, k, True)
    send_tiles(pm)
    send_last_plane(ps)
    loads[4].wait()
    parts(ps, 0, True)
    send_first_plane(ps)
    for k in range(1, NPL):
        parts(ps, k, True)
    send_tiles(ps)
    loads[5].wait()
    loads[6].wait()

    def adjoint_mid(k, j):
        rows, out = spots(j)
        g = slopes(v_m, k, j)
        t = g[0] * g[0] + g[1] * g[1] + g[2] * g[2] + DELTA
        rn = lax.rsqrt(t)
        n = t * rn
        w = weight[k, out]
        r = 1.0 / (w + TAU * n)
        h = w * r
        c = [cot[a, k, out] for a in range(3)]
        s = None
        for a in range(3):
            term = c[a] * (q_all[pm, a, k + 1, rows] + TAU * g[a])
            s = term if s is None else s + term
        m = TAU * r * (h * s)
        wacc[k, out] = m * n
        f = m * rn
        for a in range(3):
            hc_a = h * c[a]
            hc[a, k, out] = hc_a
            q_all[cm, a, k + 1, rows] = TAU * hc_a - f * g[a]

    step(pm, v_m, adjoint_mid, cm)

    receive_tiles(ps)
    for k in range(NPL):
        fix(ps, v_s, k)
    fix_beyond(ps, v_s)

    def prepare_start(k, j):
        rows, out = spots(j)
        g = slopes(v_s, k, j)
        t = g[0] * g[0] + g[1] * g[1] + g[2] * g[2] + DELTA
        rn = lax.rsqrt(t)
        n = t * rn
        w = weight[k, out]
        r = 1.0 / (w + TAU * n)
        h = w * r
        a1 = TAU * r * h
        aux[0, k, out] = h
        aux[1, k, out] = a1 * rn
        aux[2, k, out] = a1 * n
        for a in range(3):
            gs[a, k, out] = g[a]

    for k in range(NPL):
        plane(prepare_start, k)

    def adjoint_start(k, j):
        rows, out = spots(j)
        d = slopes(v_m, k, j)
        h = aux[0, k, out]
        g = [gs[a, k, out] for a in range(3)]
        c = [hc[a, k, out] + d[a] for a in range(3)]
        s = None
        for a in range(3):
            term = c[a] * (q_all[ps, a, k + 1, rows] + TAU * g[a])
            s = term if s is None else s + term
        wacc[k, out] = wacc[k, out] + aux[2, k, out] * s
        f = aux[1, k, out] * s
        for a in range(3):
            hc_a = h * c[a]
            hc[a, k, out] = hc_a
            q_all[cs, a, k + 1, rows] = TAU * hc_a - f * g[a]

    step(cm, v_m, adjoint_start, cs)

    def finish_weight(k, j):
        _, out = spots(j)
        wg_o[k, out] = wacc[k, out] / weight[k, out]

    for k in range(NPL):
        plane(finish_weight, k)
    receive_tiles(cs)

    def finish(k, j):
        _, out = spots(j)
        d = slopes(v_s, k, j)
        for a in range(3):
            dual_o[a, k, out] = hc[a, k, out] + d[a]
        dg_o[k, out] = KAPPA * (v_s[k, out] + v_m[k, out])

    for k in (1, 2, 3):
        fix(cs, v_s, k)
    plane(finish, 1)
    plane(finish, 2)
    fix(cs, v_s, 0)
    plane(finish, 0)
    fix_beyond(cs, v_s)
    plane(finish, 3)
    for e in range(4):
        tiles_done(e, send_sem)
        pl.when(up_z)(lambda: message(e, 10).wait_send())
        pl.when(low_z)(lambda: message(e, 11).wait_send())


def write_out(*refs):
    sem = refs[-1]
    copies = [pltpu.make_async_copy(refs[i], refs[i + 3], sem.at[i]) for i in range(3)]
    for c in copies:
        c.start()
    for c in copies:
        c.wait()


def shards(sizes, data, weight, dual_start, dual_mid, cotangent):
    field = (NPL, NRW, NCL)
    vm = pltpu.VMEM
    whole = pl.BlockSpec(memory_space=pltpu.VMEM)
    shapes = (
        jax.ShapeDtypeStruct((3,) + field, F32),
        jax.ShapeDtypeStruct(field, F32),
        jax.ShapeDtypeStruct(field, F32),
    )
    args = (data, weight, dual_start, dual_mid, cotangent)
    results = pl.pallas_call(
        functools.partial(kernel, sizes),
        out_shape=shapes,
        in_specs=[pl.BlockSpec(memory_space=pl.ANY)] * 5,
        out_specs=(whole,) * 3,
        scratch_shapes=[
            vm(field, F32),
            vm(field, F32),
            vm((3,) + field, F32),
            vm((4, 3, NPL + 1, NRW + PAD, NCL), F32),
            vm((4,) + field, F32),
            vm((NPL + 1, NRW + PAD, NCL), F32),
            vm((NPL + 1, NRW + PAD, NCL), F32),
            vm((3,) + field, F32),
            vm((3,) + field, F32),
            vm((3,) + field, F32),
            vm(field, F32),
            vm((NRW, NCL), F32),
            vm((NRW, NCL), F32),
            vm((8, NCL), F32),
            vm((4, 24, NCL), F32),
            vm((4, 10, 8, NCL), F32),
            vm((4, 2, NRW, NCL), F32),
            vm((4, 10, 8, NCL), F32),
            pltpu.SemaphoreType.DMA((7,)),
            pltpu.SemaphoreType.DMA((4, 3)),
            pltpu.SemaphoreType.DMA((4, 3)),
        ],
        compiler_params=pltpu.CompilerParams(
            collective_id=0, has_side_effects=True, vmem_limit_bytes=40 * 1024 * 1024
        ),
    )(*[pltpu.with_memory_space_constraint(x, pltpu.HBM) for x in args])
    return pl.pallas_call(
        write_out,
        out_shape=shapes,
        in_specs=[pl.BlockSpec(memory_space=pltpu.VMEM)] * 3,
        out_specs=(pl.BlockSpec(memory_space=pl.ANY),) * 3,
        scratch_shapes=[pltpu.SemaphoreType.DMA((3,))],
    )(*[pltpu.with_memory_space_constraint(x, pltpu.VMEM) for x in results])


def solution(mesh):
    field, triple = P("gz", "gx", "gy"), P(None, "gz", "gx", "gy")
    sizes = tuple(mesh.shape[a] for a in AXES)
    return jax.shard_map(
        functools.partial(shards, sizes),
        mesh=mesh,
        in_specs=(field, field, triple, triple, triple),
        out_specs=(triple, field, field),
        check_vma=False,
    )
```

```python
import functools

import jax
import jax.numpy as jnp
from jax import lax
from jax.experimental import pallas as pl
from jax.experimental.pallas import tpu as pltpu
from jax.sharding import PartitionSpec as P

MESH = pl.DeviceIdType.MESH
TAU = 0.08
KAPPA = 0.5
DELTA = 0.01
AXES = ("gx", "gy", "gz")

NPL, NRW, NCL = 4, 128, 128
CH = 32
PAD = 8
R, Z, C = 0, 1, 2
SLOTS = (
    ((-1, 0, 0), R),
    ((1, 0, 0), R),
    ((0, -1, 0), C),
    ((0, 1, 0), C),
    ((-1, 0, 1), R),
    ((1, 0, -1), Z),
    ((0, -1, 1), C),
    ((0, 1, -1), Z),
    ((1, -1, 0), C),
    ((-1, 1, 0), R),
    ((0, 0, -1), None),
    ((0, 0, 1), None),
)
NS = len(SLOTS)
F32 = jnp.float32


def kernel(
    sizes,
    data_h, weight_h, ps_h, pm_h, cot_h,
    hc_o, wg_o, u_o, dm_o, t_o, r_o, edge_o,
    data, weight, cot, q_all, u, v_m, v_s, gs, bs, aux, wacc, scale, inner, xbuf, tbuf, rbuf, tile, rcv, pln, spare,
    in_sem, send_sem, recv_sem,
):
    pos = tuple(lax.axis_index(a) for a in AXES)
    pm, ps, cm, cs = 0, 1, 2, 3
    rest = slice(1, NPL)
    loads = [
        pltpu.make_async_copy(pm_h, q_all.at[pm, :, 1 : NPL + 1, PAD : PAD + NRW], in_sem.at[0]),
        pltpu.make_async_copy(data_h, data, in_sem.at[1]),
    ]
    loads.append(pltpu.make_async_copy(ps_h, q_all.at[ps, :, 1 : NPL + 1, PAD : PAD + NRW], in_sem.at[2]))
    loads.append(pltpu.make_async_copy(weight_h, weight, in_sem.at[3]))
    loads.append(pltpu.make_async_copy(cot_h, cot, in_sem.at[4]))
    for c in loads:
        c.start()

    lane = lax.broadcasted_iota(jnp.int32, (CH, NCL), 1)
    lane8 = lax.broadcasted_iota(jnp.int32, (NPL, NCL), 1)
    sub4 = lax.broadcasted_iota(jnp.int32, (NPL, NCL), 0)

    low_x, low_y, low_z = (p > 0 for p in pos)
    up_x, up_y, up_z = (p < n - 1 for p, n in zip(pos, sizes))

    def exists(off):
        ok = None
        for o, low, up in zip(off, (low_x, low_y, low_z), (up_x, up_y, up_z)):
            if o != 0:
                here = low if o < 0 else up
                ok = here if ok is None else jnp.logical_and(ok, here)
        return ok

    has = [exists(off) for off, _ in SLOTS]
    takes = [exists(tuple(-o for o in off)) for off, _ in SLOTS]
    barrier = pltpu.get_barrier_semaphore()
    for (off, _), here in zip(SLOTS, has):
        @pl.when(here)
        def _():
            peer = tuple(p + o for p, o in zip(pos, off))
            pl.semaphore_signal(barrier, inc=1, device_id=peer, device_id_type=MESH)

    for side, here in ((0, low_z), (1, up_z)):
        @pl.when(jnp.logical_not(here))
        def _():
            for e in range(4):
                pln[e, side] = jnp.zeros((NRW, NCL), F32)

    for e in range(4):
        q_all[e, 0, 0, PAD : PAD + NRW] = jnp.zeros((NRW, NCL), F32)
        for k in range(NPL):
            q_all[e, 1, k + 1, 0:PAD] = jnp.zeros((PAD, NCL), F32)


    def message(e, s):
        off, kind = SLOTS[s]
        if kind is None:
            first = (pm_h.at[0, NPL - 1], ps_h.at[0, NPL - 1], q_all.at[cm, 0, NPL, PAD : PAD + NRW],
                     q_all.at[cs, 0, NPL, PAD : PAD + NRW])
            src = first[e] if s == 10 else u.at[e, 0]
            dst, sem = pln.at[e, s - 10], s - 9
        else:
            src, dst, sem = tile.at[e, 8 * kind : 8 * kind + 8], rcv.at[e, s], 0
        return pltpu.make_async_remote_copy(
            src_ref=src, dst_ref=dst, send_sem=send_sem.at[e, sem], recv_sem=recv_sem.at[e, sem],
            device_id=tuple(p - o for p, o in zip(pos, off)), device_id_type=MESH,
        )

    def filler(e, s, sem):
        kind = SLOTS[s][1]
        dst = rcv.at[e, s] if sem is recv_sem else spare.at[e, s]
        return pltpu.make_async_copy(tile.at[e, 8 * kind : 8 * kind + 8], dst, sem.at[e, 0])

    def tiles_done(e, sem):
        pltpu.make_async_copy(rcv.at[e], rcv.at[e], sem.at[e, 0]).wait()

    def divide_part(e, k, j, extra):
        rows = slice(PAD + CH * j, PAD + CH * (j + 1))
        above = slice(PAD + CH * j - 1, PAD + CH * (j + 1) - 1)
        out = slice(CH * j, CH * (j + 1))
        q2 = q_all[e, 2, k + 1, rows]
        total = q_all[e, 0, k + 1, rows] - q_all[e, 0, k, rows]
        total = total + (q_all[e, 1, k + 1, rows] - q_all[e, 1, k + 1, above])
        total = total + (q2 - jnp.where(lane == 0, 0.0, pltpu.roll(q2, 1, 1)))
        if extra:
            total = total - KAPPA * data[k, out]
        u[e, k, out] = total
        x = jnp.where(lane == k, pltpu.roll(q2, k + 1, 1), xbuf[out])
        xbuf[out] = jnp.where(lane == k + NPL, pltpu.roll(total, k + NPL, 1), x)

    def send_last_plane(e):
        pl.when(up_z)(lambda: message(e, 10).start())

    def send_first_plane(e):
        pl.when(low_z)(lambda: message(e, 11).start())

    def pack_tiles(e):
        for j in range(NRW // CH):
            rows = slice(PAD + CH * j, PAD + CH * (j + 1))
            out = slice(CH * j, CH * (j + 1))
            xbuf[out] = jnp.where(lane == 8, pltpu.roll(q_all[e, 0, NPL, rows], 8, 1), xbuf[out])
        xt = jnp.transpose(xbuf[...])
        tile[e, 16:24] = xt[0:8]
        tile[e, 9:10] = xt[8:9]
        tile[e, 8:9] = q_all[e, 0, NPL, PAD : PAD + 1]
        for k in range(NPL):
            tile[e, k : k + 1] = q_all[e, 1, k + 1, PAD + NRW - 1 : PAD + NRW]
            tile[e, k + NPL : k + NPL + 1] = u[e, k, 0:1]
    def send_tiles(e):
        for s in (6, 7, 8, 9, 2, 3, 4, 5, 0, 1):
            pl.when(takes[s])(lambda: message(e, s).start())
            pl.when(jnp.logical_not(takes[s]))(lambda: filler(e, s, send_sem).start())
            pl.when(jnp.logical_not(has[s]))(lambda: filler(e, s, recv_sem).start())

    def receive_tiles(e):
        tiles_done(e, recv_sem)
        low_c = jnp.where(low_y, rcv[e, 2, 0:NPL], 0.0)
        high_c = rcv[e, 3, NPL : 2 * NPL] - tile[e, 16 : 16 + NPL]
        high_c = high_c - jnp.where(jnp.logical_and(sub4 == 0, low_z), rcv[e, 7, 1:2], 0.0)
        high_c = high_c - jnp.where(jnp.logical_and(lane8 == 0, low_x), rcv[e, 9, 0:NPL], 0.0)
        tbuf[0:NPL] = low_c
        tbuf[NPL : 2 * NPL] = jnp.where(up_y, high_c, 0.0)
        tbuf[8:16] = jnp.where(low_y, rcv[e, 6], 0.0)
        tbuf[...] = jnp.transpose(tbuf[...])
        high_r = rcv[e, 1, NPL : 2 * NPL] - tile[e, 0:NPL]
        high_r = high_r - jnp.where(jnp.logical_and(sub4 == 0, low_z), rcv[e, 5, 0:1], 0.0)
        high_r = high_r - jnp.where(jnp.logical_and(lane8 == 0, low_y), rcv[e, 8, 0:NPL], 0.0)
        rbuf[0:NPL] = jnp.where(low_x, rcv[e, 0, 0:NPL], 0.0)
        rbuf[NPL : 2 * NPL] = jnp.where(up_x, high_r, 0.0)

    def fix(e, v, k):
        if k == 0:
            pl.when(low_z)(lambda: message(e, 10).wait_recv())
        for j in range(NRW // CH):
            out = slice(CH * j, CH * (j + 1))
            total = u[e, k, out] - jnp.where(lane == 0, pltpu.roll(tbuf[out], (NCL - k) % NCL, 1), 0.0)
            if k == 0:
                total = total - pln[e, 0, out]
            v[k, out] = total
        v[k, 0:1] = v[k, 0:1] - rbuf[k : k + 1]
        v[k, NRW : NRW + 1] = rbuf[NPL + k : NPL + k + 1]

    def fix_beyond(e, v):
        pl.when(up_z)(lambda: message(e, 11).wait_recv())
        for j in range(NRW // CH):
            rows = slice(PAD + CH * j, PAD + CH * (j + 1))
            out = slice(CH * j, CH * (j + 1))
            col = jnp.where(lane == 0, pltpu.roll(tbuf[out], NCL - 8, 1), 0.0)
            v[NPL, out] = jnp.where(up_z, pln[e, 1, out] - q_all[e, 0, NPL, rows] - col, 0.0)
        v[NPL, 0:1] = v[NPL, 0:1] - jnp.where(jnp.logical_and(up_z, low_x), rcv[e, 4, 0:1], 0.0)

    def slopes(v, k, j):
        out = slice(CH * j, CH * (j + 1))
        c = v[k, out]
        col = pltpu.roll(tbuf[out], NCL - 1 - NPL - k, 1)
        return (
            v[k + 1, out] - c,
            v[k, CH * j + 1 : CH * (j + 1) + 1] - c,
            jnp.where(lane == NCL - 1, col, pltpu.roll(c, NCL - 1, 1)) - c,
        )

    def plane(body, k):
        for j in range(NRW // CH):
            body(k, j)

    def parts(e, k, extra=False):
        plane(lambda k, j: divide_part(e, k, j, extra), k)

    def spots(j):
        return slice(PAD + CH * j, PAD + CH * (j + 1)), slice(CH * j, CH * (j + 1))

    def step(e, v, body, nxt):
        receive_tiles(e)
        fix(e, v, 3)
        fix_beyond(e, v)
        plane(body, 3)
        send_last_plane(nxt)
        fix(e, v, 0)
        fix(e, v, 1)
        plane(body, 0)
        parts(nxt, 0)
        send_first_plane(nxt)
        fix(e, v, 2)
        for k in (1, 2):
            plane(body, k)
            parts(nxt, k)
        parts(nxt, 3)
        pack_tiles(nxt)
        send_tiles(nxt)

    for k in range(NPL):
        if k == 0:
            loads[0].wait()
            loads[1].wait()
        parts(pm, k, True)
    pack_tiles(pm)
    pl.semaphore_wait(barrier, sum(jnp.where(here, 1, 0) for here in has))
    send_last_plane(pm)
    send_first_plane(pm)
    send_tiles(pm)
    send_last_plane(ps)
    loads[2].wait()
    parts(ps, 0, True)
    send_first_plane(ps)
    for k in range(1, NPL):
        parts(ps, k, True)
    pack_tiles(ps)
    send_tiles(ps)
    loads[3].wait()
    loads[4].wait()

    def multiply_mid(k, j):
        rows, out = spots(j)
        s = None
        for a in range(3):
            term = cot[a, k, out] * q_all[pm, a, k + 1, rows]
            s = term if s is None else s + term
        inner[k, out] = s

    for k in range(NPL):
        plane(multiply_mid, k)

    def weights(g, w):
        t = g[0] * g[0] + g[1] * g[1] + g[2] * g[2] + DELTA
        rn = lax.rsqrt(t)
        n = t * rn
        r = 1.0 / (w + TAU * n)
        return rn, n, w * r, TAU * r

    def adjoint_mid(k, j):
        rows, out = spots(j)
        g = slopes(v_m, k, j)
        rn, n, h, tr = weights(g, weight[k, out])
        c = [cot[a, k, out] for a in range(3)]
        s = inner[k, out] + TAU * (c[0] * g[0] + c[1] * g[1] + c[2] * g[2])
        m = tr * (h * s)
        f = m * rn
        th = TAU * h
        for a in range(3):
            q_all[cm, a, k + 1, rows] = th * c[a] - f * g[a]
        wacc[k, out] = m * n
        scale[k, out] = h

    step(pm, v_m, adjoint_mid, cm)

    receive_tiles(ps)
    for k in range(NPL):
        fix(ps, v_s, k)
    fix_beyond(ps, v_s)

    def prepare_start(k, j):
        rows, out = spots(j)
        for a in range(3):
            hc_o[a, k, out] = scale[k, out] * cot[a, k, out]
        g = slopes(v_s, k, j)
        rn, n, h, tr = weights(g, weight[k, out])
        a1 = tr * h
        aux[0, k, out] = TAU * h
        aux[1, k, out] = a1 * rn
        aux[2, k, out] = a1 * n
        scale[k, out] = h
        for a in range(3):
            gs[a, k, out] = g[a]
            bs[a, k, out] = q_all[ps, a, k + 1, rows] + TAU * g[a]

    for k in range(NPL):
        plane(prepare_start, k)

    def adjoint_start(k, j):
        rows, out = spots(j)
        d = slopes(v_m, k, j)
        c = [hc_o[a, k, out] + d[a] for a in range(3)]
        s = c[0] * bs[0, k, out] + c[1] * bs[1, k, out] + c[2] * bs[2, k, out]
        f = aux[1, k, out] * s
        th = aux[0, k, out]
        for a in range(3):
            q_all[cs, a, k + 1, rows] = th * c[a] - f * gs[a, k, out]
            hc_o[a, k, out] = c[a]
        inner[k, out] = s

    step(cm, v_m, adjoint_start, cs)

    def finish_weight(k, j):
        _, out = spots(j)
        wg_o[k, out] = (wacc[k, out] + aux[2, k, out] * inner[k, out]) / weight[k, out]
        for a in range(3):
            hc_o[a, k, out] = scale[k, out] * hc_o[a, k, out]
        dm_o[k, out] = v_m[k, out]
        u_o[k, out] = u[cs, k, out]

    for k in range(NPL):
        plane(finish_weight, k)
    receive_tiles(cs)
    t_o[...] = tbuf[...]
    r_o[...] = rbuf[...]
    fix_beyond(cs, v_s)
    edge_o[1] = v_s[NPL, 0:NRW]
    pl.when(low_z)(lambda: message(cs, 10).wait_recv())
    edge_o[0] = pln[cs, 0]
    for e in range(4):
        tiles_done(e, send_sem)
        pl.when(up_z)(lambda: message(e, 10).wait_send())
        pl.when(low_z)(lambda: message(e, 11).wait_send())


def finish(hc, wg, u, dm, tcol, rrow, edge, dual_h, wg_h, dg_h, v, dual, dg, sem):
    lane = lax.broadcasted_iota(jnp.int32, (CH, NCL), 1)
    copies = [pltpu.make_async_copy(wg, wg_h, sem.at[0])]
    copies[0].start()
    v[NPL, 0:NRW] = edge[1]
    for k in reversed(range(NPL)):
        for j in range(NRW // CH):
            out = slice(CH * j, CH * (j + 1))
            total = u[k, out] - jnp.where(lane == 0, pltpu.roll(tcol[out], (NCL - k) % NCL, 1), 0.0)
            if k == 0:
                total = total - edge[0, out]
            v[k, out] = total
        v[k, 0:1] = v[k, 0:1] - rrow[k : k + 1]
        v[k, NRW : NRW + 1] = rrow[NPL + k : NPL + k + 1]
        for j in range(NRW // CH):
            out = slice(CH * j, CH * (j + 1))
            c = v[k, out]
            col = pltpu.roll(tcol[out], NCL - 1 - NPL - k, 1)
            dual[0, k, out] = hc[0, k, out] + (v[k + 1, out] - c)
            dual[1, k, out] = hc[1, k, out] + (v[k, CH * j + 1 : CH * (j + 1) + 1] - c)
            dual[2, k, out] = hc[2, k, out] + (jnp.where(lane == NCL - 1, col, pltpu.roll(c, NCL - 1, 1)) - c)
            dg[k, out] = KAPPA * (c + dm[k, out])
        here = [
            pltpu.make_async_copy(dual.at[:, k], dual_h.at[:, k], sem.at[2 * k + 1]),
            pltpu.make_async_copy(dg.at[k], dg_h.at[k], sem.at[2 * k + 2]),
        ]
        for c in here:
            c.start()
        copies += here
    for c in copies:
        c.wait()


def shards(sizes, data, weight, dual_start, dual_mid, cotangent):
    field = (NPL, NRW, NCL)
    vm = pltpu.VMEM
    whole = pl.BlockSpec(memory_space=pltpu.VMEM)
    shapes = (
        jax.ShapeDtypeStruct((3,) + field, F32),
        jax.ShapeDtypeStruct(field, F32),
        jax.ShapeDtypeStruct(field, F32),
    )
    args = (data, weight, dual_start, dual_mid, cotangent)
    face = (NRW, NCL)
    between = ((3,) + field, field, field, field, face, (8, NCL), (2,) + face)
    results = pl.pallas_call(
        functools.partial(kernel, sizes),
        out_shape=[jax.ShapeDtypeStruct(x, F32) for x in between],
        in_specs=[pl.BlockSpec(memory_space=pl.ANY)] * 5,
        out_specs=[whole] * len(between),
        scratch_shapes=[
            vm(field, F32),
            vm(field, F32),
            vm((3,) + field, F32),
            vm((4, 3, NPL + 1, NRW + PAD, NCL), F32),
            vm((4,) + field, F32),
            vm((NPL + 1, NRW + PAD, NCL), F32),
            vm((NPL + 1, NRW + PAD, NCL), F32),
            vm((3,) + field, F32),
            vm((3,) + field, F32),
            vm((3,) + field, F32),
            vm(field, F32),
            vm(field, F32),
            vm(field, F32),
            vm((NRW, NCL), F32),
            vm((NRW, NCL), F32),
            vm((8, NCL), F32),
            vm((4, 24, NCL), F32),
            vm((4, 10, 8, NCL), F32),
            vm((4, 2, NRW, NCL), F32),
            vm((4, 10, 8, NCL), F32),
            pltpu.SemaphoreType.DMA((5,)),
            pltpu.SemaphoreType.DMA((4, 3)),
            pltpu.SemaphoreType.DMA((4, 3)),
        ],
        compiler_params=pltpu.CompilerParams(
            collective_id=0, has_side_effects=True, vmem_limit_bytes=40 * 1024 * 1024
        ),
    )(*[pltpu.with_memory_space_constraint(x, pltpu.HBM) for x in args])
    return pl.pallas_call(
        finish,
        out_shape=shapes,
        in_specs=[whole] * len(between),
        out_specs=(pl.BlockSpec(memory_space=pl.ANY),) * 3,
        scratch_shapes=[
            vm((NPL + 1, NRW + PAD, NCL), F32),
            vm((3,) + field, F32),
            vm(field, F32),
            pltpu.SemaphoreType.DMA((9,)),
        ],
    )(*[pltpu.with_memory_space_constraint(x, pltpu.VMEM) for x in results])


def solution(mesh):
    field, triple = P("gz", "gx", "gy"), P(None, "gz", "gx", "gy")
    sizes = tuple(mesh.shape[a] for a in AXES)
    return jax.shard_map(
        functools.partial(shards, sizes),
        mesh=mesh,
        in_specs=(field, field, triple, triple, triple),
        out_specs=(triple, field, field),
        check_vma=False,
    )
```

```python
import functools

import jax
import jax.numpy as jnp
from jax import lax
from jax.experimental import pallas as pl
from jax.experimental.pallas import tpu as pltpu
from jax.sharding import PartitionSpec as P

MESH = pl.DeviceIdType.MESH
TAU = 0.08
KAPPA = 0.5
DELTA = 0.01
AXES = ("gx", "gy", "gz")

NPL, NRW, NCL = 4, 128, 128
CH = 32
PAD = 8
R, Z, C = 0, 1, 2
SLOTS = (
    ((-1, 0, 0), R),
    ((1, 0, 0), R),
    ((0, -1, 0), C),
    ((0, 1, 0), C),
    ((-1, 0, 1), R),
    ((1, 0, -1), Z),
    ((0, -1, 1), C),
    ((0, 1, -1), Z),
    ((1, -1, 0), C),
    ((-1, 1, 0), R),
    ((0, 0, -1), None),
    ((0, 0, 1), None),
)
NS = len(SLOTS)
F32 = jnp.float32


def kernel(
    sizes,
    data_h, weight_h, ps_h, pm_h, cot_h,
    hc_o, wg_o, u_o, dm_o, t_o, r_o, edge_o,
    data, weight, cot, q_all, u, v_m, v_s, gs, bs, aux, wacc, scale, inner, xbuf, tbuf, cols, rbuf, tile, rcv, pln, spare,
    in_sem, send_sem, recv_sem,
):
    pos = tuple(lax.axis_index(a) for a in AXES)
    pm, ps, cm, cs = 0, 1, 2, 3
    rest = slice(1, NPL)
    loads = [
        pltpu.make_async_copy(pm_h, q_all.at[pm, :, 1 : NPL + 1, PAD : PAD + NRW], in_sem.at[0]),
        pltpu.make_async_copy(data_h, data, in_sem.at[1]),
    ]
    loads.append(pltpu.make_async_copy(ps_h, q_all.at[ps, :, 1 : NPL + 1, PAD : PAD + NRW], in_sem.at[2]))
    loads.append(pltpu.make_async_copy(weight_h, weight, in_sem.at[3]))
    loads.append(pltpu.make_async_copy(cot_h, cot, in_sem.at[4]))
    for c in loads:
        c.start()

    lane = lax.broadcasted_iota(jnp.int32, (CH, NCL), 1)
    lane8 = lax.broadcasted_iota(jnp.int32, (8, NCL), 1)
    sub8 = lax.broadcasted_iota(jnp.int32, (8, NCL), 0)
    odd = sub8 % 2 == 1

    low_x, low_y, low_z = (p > 0 for p in pos)
    up_x, up_y, up_z = (p < n - 1 for p, n in zip(pos, sizes))

    def exists(off):
        ok = None
        for o, low, up in zip(off, (low_x, low_y, low_z), (up_x, up_y, up_z)):
            if o != 0:
                here = low if o < 0 else up
                ok = here if ok is None else jnp.logical_and(ok, here)
        return ok

    has = [exists(off) for off, _ in SLOTS]
    takes = [exists(tuple(-o for o in off)) for off, _ in SLOTS]
    barrier = pltpu.get_barrier_semaphore()
    for (off, _), here in zip(SLOTS, has):
        @pl.when(here)
        def _():
            peer = tuple(p + o for p, o in zip(pos, off))
            pl.semaphore_signal(barrier, inc=1, device_id=peer, device_id_type=MESH)

    for side, here in ((0, low_z), (1, up_z)):
        @pl.when(jnp.logical_not(here))
        def _():
            for e in range(4):
                pln[e, side] = jnp.zeros((NRW, NCL), F32)

    for e in range(4):
        q_all[e, 0, 0, PAD : PAD + NRW] = jnp.zeros((NRW, NCL), F32)
        for k in range(NPL):
            q_all[e, 1, k + 1, 0:PAD] = jnp.zeros((PAD, NCL), F32)


    def message(e, s):
        off, kind = SLOTS[s]
        if kind is None:
            first = (pm_h.at[0, NPL - 1], ps_h.at[0, NPL - 1], q_all.at[cm, 0, NPL, PAD : PAD + NRW],
                     q_all.at[cs, 0, NPL, PAD : PAD + NRW])
            src = first[e] if s == 10 else u.at[e, 0]
            dst, sem = pln.at[e, s - 10], s - 9
        else:
            src, dst, sem = tile.at[e, 8 * kind : 8 * kind + 8], rcv.at[e, s], 0
        return pltpu.make_async_remote_copy(
            src_ref=src, dst_ref=dst, send_sem=send_sem.at[e, sem], recv_sem=recv_sem.at[e, sem],
            device_id=tuple(p - o for p, o in zip(pos, off)), device_id_type=MESH,
        )

    def filler(e, s, sem):
        kind = SLOTS[s][1]
        dst = rcv.at[e, s] if sem is recv_sem else spare.at[e, s]
        return pltpu.make_async_copy(tile.at[e, 8 * kind : 8 * kind + 8], dst, sem.at[e, 0])

    def tiles_done(e, sem):
        pltpu.make_async_copy(rcv.at[e], rcv.at[e], sem.at[e, 0]).wait()

    def divide_part(e, k, j, extra):
        rows = slice(PAD + CH * j, PAD + CH * (j + 1))
        above = slice(PAD + CH * j - 1, PAD + CH * (j + 1) - 1)
        out = slice(CH * j, CH * (j + 1))
        q2 = q_all[e, 2, k + 1, rows]
        total = q_all[e, 0, k + 1, rows] - q_all[e, 0, k, rows]
        total = total + (q_all[e, 1, k + 1, rows] - q_all[e, 1, k + 1, above])
        total = total + (q2 - jnp.where(lane == 0, 0.0, pltpu.roll(q2, 1, 1)))
        if extra:
            total = total - KAPPA * data[k, out]
        u[e, k, out] = total
        ends = pltpu.roll(jnp.where(lane < NCL // 2, total, q2), 2 * k + 1, 1)
        xbuf[out] = jnp.where(lane // 2 == k, ends, xbuf[out])

    def send_last_plane(e):
        pl.when(up_z)(lambda: message(e, 10).start())

    def send_first_plane(e):
        pl.when(low_z)(lambda: message(e, 11).start())

    def pack_tiles(e):
        for j in range(NRW // CH):
            rows = slice(PAD + CH * j, PAD + CH * (j + 1))
            out = slice(CH * j, CH * (j + 1))
            xbuf[out] = jnp.where(lane == 8, pltpu.roll(q_all[e, 0, NPL, rows], 8, 1), xbuf[out])
        xt = jnp.transpose(xbuf[...])
        tile[e, 16:24] = xt[0:8]
        tile[e, 9:10] = xt[8:9]
        tile[e, 8:9] = q_all[e, 0, NPL, PAD : PAD + 1]
        for k in range(NPL):
            tile[e, 2 * k : 2 * k + 1] = q_all[e, 1, k + 1, PAD + NRW - 1 : PAD + NRW]
            tile[e, 2 * k + 1 : 2 * k + 2] = u[e, k, 0:1]
    def send_tiles(e):
        for s in (6, 7, 8, 9, 2, 3, 4, 5, 0, 1):
            pl.when(takes[s])(lambda: message(e, s).start())
            pl.when(jnp.logical_not(takes[s]))(lambda: filler(e, s, send_sem).start())
            pl.when(jnp.logical_not(has[s]))(lambda: filler(e, s, recv_sem).start())

    def receive_tiles(e):
        tiles_done(e, recv_sem)
        high_c = pltpu.roll(rcv[e, 3], 7, 0) - tile[e, 16:24]
        high_c = high_c - jnp.where(jnp.logical_and(sub8 == 0, low_z), rcv[e, 7, 1:2], 0.0)
        high_c = high_c - jnp.where(jnp.logical_and(lane8 == 0, low_x), rcv[e, 9], 0.0)
        high_c = jnp.where(up_y, high_c, 0.0)
        low_c = jnp.where(low_y, pltpu.roll(rcv[e, 2], 1, 0), 0.0)
        tbuf[0:8] = jnp.where(odd, low_c, high_c)
        tbuf[8:16] = jnp.where(low_y, rcv[e, 6], 0.0)
        tbuf[...] = jnp.transpose(tbuf[...])
        high_r = pltpu.roll(rcv[e, 1], 7, 0) - tile[e, 0:8]
        high_r = high_r - jnp.where(jnp.logical_and(sub8 == 0, low_z), rcv[e, 5, 0:1], 0.0)
        high_r = high_r - jnp.where(jnp.logical_and(lane8 == 0, low_y), rcv[e, 8], 0.0)
        high_r = jnp.where(up_x, high_r, 0.0)
        low_r = jnp.where(low_x, pltpu.roll(rcv[e, 0], 1, 0), 0.0)
        rbuf[...] = jnp.where(odd, low_r, high_r)

    def receive_planes(e):
        pl.when(low_z)(lambda: message(e, 10).wait_recv())
        pl.when(up_z)(lambda: message(e, 11).wait_recv())

    def fix(e, v, k):
        for j in range(NRW // CH):
            out = slice(CH * j, CH * (j + 1))
            col = pltpu.roll(tbuf[out], NCL - 2 * k - 1, 1)
            cols[k, out] = col
            total = u[e, k, out] - jnp.where(lane == 0, col, 0.0)
            if k == 0:
                total = total - pln[e, 0, out]
            v[k, out] = total
        v[k, 0:1] = v[k, 0:1] - rbuf[2 * k + 1 : 2 * k + 2]
        v[k, NRW : NRW + 1] = rbuf[2 * k : 2 * k + 1]

    def fix_beyond(e, v):
        for j in range(NRW // CH):
            rows = slice(PAD + CH * j, PAD + CH * (j + 1))
            out = slice(CH * j, CH * (j + 1))
            col = jnp.where(lane == 0, pltpu.roll(tbuf[out], NCL - 8, 1), 0.0)
            v[NPL, out] = jnp.where(up_z, pln[e, 1, out] - q_all[e, 0, NPL, rows] - col, 0.0)
        v[NPL, 0:1] = v[NPL, 0:1] - jnp.where(jnp.logical_and(up_z, low_x), rcv[e, 4, 0:1], 0.0)

    def slopes(v, k, j):
        out = slice(CH * j, CH * (j + 1))
        c = v[k, out]
        col = cols[k, out]
        return (
            v[k + 1, out] - c,
            v[k, CH * j + 1 : CH * (j + 1) + 1] - c,
            jnp.where(lane == NCL - 1, col, pltpu.roll(c, NCL - 1, 1)) - c,
        )

    def plane(body, k):
        for j in range(NRW // CH):
            body(k, j)

    def parts(e, k, extra=False):
        plane(lambda k, j: divide_part(e, k, j, extra), k)

    def spots(j):
        return slice(PAD + CH * j, PAD + CH * (j + 1)), slice(CH * j, CH * (j + 1))

    def step(e, v, body, nxt):
        receive_tiles(e)
        receive_planes(e)
        fix(e, v, 3)
        fix(e, v, 1)
        fix(e, v, 0)
        fix_beyond(e, v)
        plane(body, 3)
        plane(body, 0)
        parts(nxt, 0)
        send_first_plane(nxt)
        send_last_plane(nxt)
        fix(e, v, 2)
        for k in (1, 2):
            plane(body, k)
            parts(nxt, k)
        parts(nxt, 3)
        pack_tiles(nxt)
        send_tiles(nxt)

    for k in range(NPL):
        if k == 0:
            loads[0].wait()
            loads[1].wait()
        parts(pm, k, True)
    pack_tiles(pm)
    pl.semaphore_wait(barrier, sum(jnp.where(here, 1, 0) for here in has))
    send_last_plane(pm)
    send_first_plane(pm)
    send_tiles(pm)
    send_last_plane(ps)
    loads[2].wait()
    parts(ps, 0, True)
    send_first_plane(ps)
    for k in range(1, NPL):
        parts(ps, k, True)
    pack_tiles(ps)
    send_tiles(ps)
    loads[3].wait()
    loads[4].wait()

    def multiply_mid(k, j):
        rows, out = spots(j)
        s = None
        for a in range(3):
            term = cot[a, k, out] * q_all[pm, a, k + 1, rows]
            s = term if s is None else s + term
        inner[k, out] = s

    for k in range(NPL):
        plane(multiply_mid, k)

    def weights(g, w):
        t = g[0] * g[0] + g[1] * g[1] + g[2] * g[2] + DELTA
        rn = lax.rsqrt(t)
        n = t * rn
        r = 1.0 / (w + TAU * n)
        return rn, n, w * r, TAU * r

    def adjoint_mid(k, j):
        rows, out = spots(j)
        g = slopes(v_m, k, j)
        rn, n, h, tr = weights(g, weight[k, out])
        c = [cot[a, k, out] for a in range(3)]
        s = inner[k, out] + TAU * (c[0] * g[0] + c[1] * g[1] + c[2] * g[2])
        m = tr * (h * s)
        f = m * rn
        th = TAU * h
        for a in range(3):
            q_all[cm, a, k + 1, rows] = th * c[a] - f * g[a]
        wacc[k, out] = m * n
        scale[k, out] = h

    step(pm, v_m, adjoint_mid, cm)

    receive_tiles(ps)
    receive_planes(ps)
    for k in range(NPL):
        fix(ps, v_s, k)
    fix_beyond(ps, v_s)

    def prepare_start(k, j):
        rows, out = spots(j)
        for a in range(3):
            hc_o[a, k, out] = scale[k, out] * cot[a, k, out]
        g = slopes(v_s, k, j)
        rn, n, h, tr = weights(g, weight[k, out])
        a1 = tr * h
        aux[0, k, out] = TAU * h
        aux[1, k, out] = a1 * rn
        aux[2, k, out] = a1 * n
        scale[k, out] = h
        for a in range(3):
            gs[a, k, out] = g[a]
            bs[a, k, out] = q_all[ps, a, k + 1, rows] + TAU * g[a]

    for k in range(NPL):
        plane(prepare_start, k)

    def adjoint_start(k, j):
        rows, out = spots(j)
        d = slopes(v_m, k, j)
        c = [hc_o[a, k, out] + d[a] for a in range(3)]
        s = c[0] * bs[0, k, out] + c[1] * bs[1, k, out] + c[2] * bs[2, k, out]
        f = aux[1, k, out] * s
        th = aux[0, k, out]
        for a in range(3):
            q_all[cs, a, k + 1, rows] = th * c[a] - f * gs[a, k, out]
            hc_o[a, k, out] = c[a]
        inner[k, out] = s

    step(cm, v_m, adjoint_start, cs)

    def finish_weight(k, j):
        _, out = spots(j)
        wg_o[k, out] = (wacc[k, out] + aux[2, k, out] * inner[k, out]) / weight[k, out]
        for a in range(3):
            hc_o[a, k, out] = scale[k, out] * hc_o[a, k, out]
        dm_o[k, out] = v_m[k, out]
        u_o[k, out] = u[cs, k, out]

    for k in range(NPL):
        plane(finish_weight, k)
    receive_tiles(cs)
    receive_planes(cs)
    t_o[...] = tbuf[...]
    r_o[...] = rbuf[...]
    fix_beyond(cs, v_s)
    edge_o[1] = v_s[NPL, 0:NRW]
    edge_o[0] = pln[cs, 0]
    for e in range(4):
        tiles_done(e, send_sem)
        pl.when(up_z)(lambda: message(e, 10).wait_send())
        pl.when(low_z)(lambda: message(e, 11).wait_send())


def finish(hc, wg, u, dm, tcol, rrow, edge, dual_h, wg_h, dg_h, v, dual, dg, sem):
    lane = lax.broadcasted_iota(jnp.int32, (CH, NCL), 1)
    copies = [pltpu.make_async_copy(wg, wg_h, sem.at[0])]
    copies[0].start()
    v[NPL, 0:NRW] = edge[1]
    for k in reversed(range(NPL)):
        for j in range(NRW // CH):
            out = slice(CH * j, CH * (j + 1))
            total = u[k, out] - jnp.where(lane == 0, pltpu.roll(tcol[out], NCL - 2 * k - 1, 1), 0.0)
            if k == 0:
                total = total - edge[0, out]
            v[k, out] = total
        v[k, 0:1] = v[k, 0:1] - rrow[2 * k + 1 : 2 * k + 2]
        v[k, NRW : NRW + 1] = rrow[2 * k : 2 * k + 1]
        for j in range(NRW // CH):
            out = slice(CH * j, CH * (j + 1))
            c = v[k, out]
            col = pltpu.roll(tcol[out], NCL - 2 * k - 1, 1)
            dual[0, k, out] = hc[0, k, out] + (v[k + 1, out] - c)
            dual[1, k, out] = hc[1, k, out] + (v[k, CH * j + 1 : CH * (j + 1) + 1] - c)
            dual[2, k, out] = hc[2, k, out] + (jnp.where(lane == NCL - 1, col, pltpu.roll(c, NCL - 1, 1)) - c)
            dg[k, out] = KAPPA * (c + dm[k, out])
        here = [
            pltpu.make_async_copy(dual.at[:, k], dual_h.at[:, k], sem.at[2 * k + 1]),
            pltpu.make_async_copy(dg.at[k], dg_h.at[k], sem.at[2 * k + 2]),
        ]
        for c in here:
            c.start()
        copies += here
    for c in copies:
        c.wait()


def shards(sizes, data, weight, dual_start, dual_mid, cotangent):
    field = (NPL, NRW, NCL)
    vm = pltpu.VMEM
    whole = pl.BlockSpec(memory_space=pltpu.VMEM)
    shapes = (
        jax.ShapeDtypeStruct((3,) + field, F32),
        jax.ShapeDtypeStruct(field, F32),
        jax.ShapeDtypeStruct(field, F32),
    )
    args = (data, weight, dual_start, dual_mid, cotangent)
    face = (NRW, NCL)
    between = ((3,) + field, field, field, field, face, (8, NCL), (2,) + face)
    results = pl.pallas_call(
        functools.partial(kernel, sizes),
        out_shape=[jax.ShapeDtypeStruct(x, F32) for x in between],
        in_specs=[pl.BlockSpec(memory_space=pl.ANY)] * 5,
        out_specs=[whole] * len(between),
        scratch_shapes=[
            vm(field, F32),
            vm(field, F32),
            vm((3,) + field, F32),
            vm((4, 3, NPL + 1, NRW + PAD, NCL), F32),
            vm((4,) + field, F32),
            vm((NPL + 1, NRW + PAD, NCL), F32),
            vm((NPL + 1, NRW + PAD, NCL), F32),
            vm((3,) + field, F32),
            vm((3,) + field, F32),
            vm((3,) + field, F32),
            vm(field, F32),
            vm(field, F32),
            vm(field, F32),
            vm((NRW, NCL), F32),
            vm((NRW, NCL), F32),
            vm(field, F32),
            vm((8, NCL), F32),
            vm((4, 24, NCL), F32),
            vm((4, 10, 8, NCL), F32),
            vm((4, 2, NRW, NCL), F32),
            vm((4, 10, 8, NCL), F32),
            pltpu.SemaphoreType.DMA((5,)),
            pltpu.SemaphoreType.DMA((4, 3)),
            pltpu.SemaphoreType.DMA((4, 3)),
        ],
        compiler_params=pltpu.CompilerParams(
            collective_id=0, has_side_effects=True, vmem_limit_bytes=40 * 1024 * 1024
        ),
    )(*[pltpu.with_memory_space_constraint(x, pltpu.HBM) for x in args])
    return pl.pallas_call(
        finish,
        out_shape=shapes,
        in_specs=[whole] * len(between),
        out_specs=(pl.BlockSpec(memory_space=pl.ANY),) * 3,
        scratch_shapes=[
            vm((NPL + 1, NRW + PAD, NCL), F32),
            vm((3,) + field, F32),
            vm(field, F32),
            pltpu.SemaphoreType.DMA((9,)),
        ],
    )(*[pltpu.with_memory_space_constraint(x, pltpu.VMEM) for x in results])


def solution(mesh):
    field, triple = P("gz", "gx", "gy"), P(None, "gz", "gx", "gy")
    sizes = tuple(mesh.shape[a] for a in AXES)
    return jax.shard_map(
        functools.partial(shards, sizes),
        mesh=mesh,
        in_specs=(field, field, triple, triple, triple),
        out_specs=(triple, field, field),
        check_vma=False,
    )
```

```python
import functools

import jax
import jax.numpy as jnp
from jax import lax
from jax.experimental import pallas as pl
from jax.experimental.pallas import tpu as pltpu
from jax.sharding import PartitionSpec as P

MESH = pl.DeviceIdType.MESH
TAU = 0.08
KAPPA = 0.5
DELTA = 0.01
AXES = ("gx", "gy", "gz")

NPL, NRW, NCL = 4, 128, 128
CH = 64
PAD = 8
R, Z, C = 0, 1, 2
SLOTS = (
    ((-1, 0, 0), R),
    ((1, 0, 0), R),
    ((0, -1, 0), C),
    ((0, 1, 0), C),
    ((-1, 0, 1), R),
    ((1, 0, -1), Z),
    ((0, -1, 1), C),
    ((0, 1, -1), Z),
    ((1, -1, 0), C),
    ((-1, 1, 0), R),
    ((0, 0, -1), None),
    ((0, 0, 1), None),
)
NS = len(SLOTS)
F32 = jnp.float32


def kernel(
    sizes,
    data_h, weight_h, ps_h, pm_h, cot_h,
    hc_o, wg_o, u_o, dm_o, t_o, r_o, edge_o,
    data, weight, cot, q_all, u, v_m, v_s, gs, bs, aux, wacc, scale, inner, xbuf, tbuf, cols, rbuf, tile, rcv, pln, spare,
    in_sem, send_sem, recv_sem,
):
    pos = tuple(lax.axis_index(a) for a in AXES)
    pm, ps, cm, cs = 0, 1, 2, 3
    rest = slice(1, NPL)
    loads = [
        pltpu.make_async_copy(pm_h, q_all.at[pm, :, 1 : NPL + 1, PAD : PAD + NRW], in_sem.at[0]),
        pltpu.make_async_copy(data_h, data, in_sem.at[1]),
    ]
    loads.append(pltpu.make_async_copy(ps_h, q_all.at[ps, :, 1 : NPL + 1, PAD : PAD + NRW], in_sem.at[2]))
    loads.append(pltpu.make_async_copy(weight_h, weight, in_sem.at[3]))
    loads.append(pltpu.make_async_copy(cot_h, cot, in_sem.at[4]))
    for c in loads:
        c.start()

    lane = lax.broadcasted_iota(jnp.int32, (CH, NCL), 1)
    row = lax.broadcasted_iota(jnp.int32, (CH, NCL), 0)
    lane8 = lax.broadcasted_iota(jnp.int32, (8, NCL), 1)
    sub8 = lax.broadcasted_iota(jnp.int32, (8, NCL), 0)
    odd = sub8 % 2 == 1

    low_x, low_y, low_z = (p > 0 for p in pos)
    up_x, up_y, up_z = (p < n - 1 for p, n in zip(pos, sizes))

    def exists(off):
        ok = None
        for o, low, up in zip(off, (low_x, low_y, low_z), (up_x, up_y, up_z)):
            if o != 0:
                here = low if o < 0 else up
                ok = here if ok is None else jnp.logical_and(ok, here)
        return ok

    has = [exists(off) for off, _ in SLOTS]
    takes = [exists(tuple(-o for o in off)) for off, _ in SLOTS]
    barrier = pltpu.get_barrier_semaphore()
    for (off, _), here in zip(SLOTS, has):
        @pl.when(here)
        def _():
            peer = tuple(p + o for p, o in zip(pos, off))
            pl.semaphore_signal(barrier, inc=1, device_id=peer, device_id_type=MESH)

    for side, here in ((0, low_z), (1, up_z)):
        @pl.when(jnp.logical_not(here))
        def _():
            for e in range(4):
                pln[e, side] = jnp.zeros((NRW, NCL), F32)

    for e in range(4):
        q_all[e, 0, 0, PAD : PAD + NRW] = jnp.zeros((NRW, NCL), F32)
        for k in range(NPL):
            q_all[e, 1, k + 1, 0:PAD] = jnp.zeros((PAD, NCL), F32)


    def message(e, s):
        off, kind = SLOTS[s]
        if kind is None:
            first = (pm_h.at[0, NPL - 1], ps_h.at[0, NPL - 1], q_all.at[cm, 0, NPL, PAD : PAD + NRW],
                     q_all.at[cs, 0, NPL, PAD : PAD + NRW])
            src = first[e] if s == 10 else u.at[e, 0]
            dst, sem = pln.at[e, s - 10], s - 9
        else:
            src, dst, sem = tile.at[e, 8 * kind : 8 * kind + 8], rcv.at[e, s], 0
        return pltpu.make_async_remote_copy(
            src_ref=src, dst_ref=dst, send_sem=send_sem.at[e, sem], recv_sem=recv_sem.at[e, sem],
            device_id=tuple(p - o for p, o in zip(pos, off)), device_id_type=MESH,
        )

    def filler(e, s, sem):
        kind = SLOTS[s][1]
        dst = rcv.at[e, s] if sem is recv_sem else spare.at[e, s]
        return pltpu.make_async_copy(tile.at[e, 8 * kind : 8 * kind + 8], dst, sem.at[e, 0])

    def tiles_done(e, sem):
        pltpu.make_async_copy(rcv.at[e], rcv.at[e], sem.at[e, 0]).wait()

    def divide_part(e, k, j, extra):
        rows = slice(PAD + CH * j, PAD + CH * (j + 1))
        above = slice(PAD + CH * j - 1, PAD + CH * (j + 1) - 1)
        out = slice(CH * j, CH * (j + 1))
        q2 = q_all[e, 2, k + 1, rows]
        total = q_all[e, 0, k + 1, rows] - q_all[e, 0, k, rows]
        total = total + (q_all[e, 1, k + 1, rows] - q_all[e, 1, k + 1, above])
        total = total + (q2 - jnp.where(lane == 0, 0.0, pltpu.roll(q2, 1, 1)))
        if extra:
            total = total - KAPPA * data[k, out]
        u[e, k, out] = total
        ends = pltpu.roll(jnp.where(lane < NCL // 2, total, q2), 2 * k + 1, 1)
        xbuf[out] = jnp.where(lane // 2 == k, ends, xbuf[out])

    def send_last_plane(e):
        pl.when(up_z)(lambda: message(e, 10).start())

    def send_first_plane(e):
        pl.when(low_z)(lambda: message(e, 11).start())

    def pack_tiles(e):
        for j in range(NRW // CH):
            rows = slice(PAD + CH * j, PAD + CH * (j + 1))
            out = slice(CH * j, CH * (j + 1))
            xbuf[out] = jnp.where(lane == 8, pltpu.roll(q_all[e, 0, NPL, rows], 8, 1), xbuf[out])
        xt = jnp.transpose(xbuf[...])
        tile[e, 16:24] = xt[0:8]
        tile[e, 9:10] = xt[8:9]
        tile[e, 8:9] = q_all[e, 0, NPL, PAD : PAD + 1]
        for k in range(NPL):
            tile[e, 2 * k : 2 * k + 1] = q_all[e, 1, k + 1, PAD + NRW - 1 : PAD + NRW]
            tile[e, 2 * k + 1 : 2 * k + 2] = u[e, k, 0:1]
    def send_tiles(e):
        for s in (6, 7, 8, 9, 2, 3, 4, 5, 0, 1):
            pl.when(takes[s])(lambda: message(e, s).start())
            pl.when(jnp.logical_not(takes[s]))(lambda: filler(e, s, send_sem).start())
            pl.when(jnp.logical_not(has[s]))(lambda: filler(e, s, recv_sem).start())

    def receive_tiles(e):
        tiles_done(e, recv_sem)
        high_c = pltpu.roll(rcv[e, 3], 7, 0) - tile[e, 16:24]
        high_c = high_c - jnp.where(jnp.logical_and(sub8 == 0, low_z), rcv[e, 7, 1:2], 0.0)
        high_c = high_c - jnp.where(jnp.logical_and(lane8 == 0, low_x), rcv[e, 9], 0.0)
        high_c = jnp.where(up_y, high_c, 0.0)
        low_c = jnp.where(low_y, pltpu.roll(rcv[e, 2], 1, 0), 0.0)
        tbuf[0:8] = jnp.where(odd, low_c, high_c)
        tbuf[8:16] = jnp.where(low_y, rcv[e, 6], 0.0)
        tbuf[...] = jnp.transpose(tbuf[...])
        high_r = pltpu.roll(rcv[e, 1], 7, 0) - tile[e, 0:8]
        high_r = high_r - jnp.where(jnp.logical_and(sub8 == 0, low_z), rcv[e, 5, 0:1], 0.0)
        high_r = high_r - jnp.where(jnp.logical_and(lane8 == 0, low_y), rcv[e, 8], 0.0)
        high_r = jnp.where(up_x, high_r, 0.0)
        low_r = jnp.where(low_x, pltpu.roll(rcv[e, 0], 1, 0), 0.0)
        rbuf[...] = jnp.where(odd, low_r, high_r)

    def receive_planes(e):
        pl.when(low_z)(lambda: message(e, 10).wait_recv())
        pl.when(up_z)(lambda: message(e, 11).wait_recv())

    def fix(e, v, k):
        for j in range(NRW // CH):
            out = slice(CH * j, CH * (j + 1))
            col = pltpu.roll(tbuf[out], NCL - 2 * k - 1, 1)
            cols[k, out] = col
            total = u[e, k, out] - jnp.where(lane == 0, col, 0.0)
            if k == 0:
                total = total - pln[e, 0, out]
            if j == 0:
                total = total - jnp.where(row == 0, rbuf[2 * k + 1 : 2 * k + 2], 0.0)
            v[k, out] = total
        v[k, NRW : NRW + 1] = rbuf[2 * k : 2 * k + 1]

    def fix_beyond(e, v):
        for j in range(NRW // CH):
            rows = slice(PAD + CH * j, PAD + CH * (j + 1))
            out = slice(CH * j, CH * (j + 1))
            col = jnp.where(lane == 0, pltpu.roll(tbuf[out], NCL - 8, 1), 0.0)
            beyond = pln[e, 1, out] - q_all[e, 0, NPL, rows] - col
            if j == 0:
                beyond = beyond - jnp.where(jnp.logical_and(row == 0, low_x), rcv[e, 4, 0:1], 0.0)
            v[NPL, out] = jnp.where(up_z, beyond, 0.0)

    def slopes(v, k, j):
        out = slice(CH * j, CH * (j + 1))
        c = v[k, out]
        col = cols[k, out]
        return (
            v[k + 1, out] - c,
            v[k, CH * j + 1 : CH * (j + 1) + 1] - c,
            jnp.where(lane == NCL - 1, col, pltpu.roll(c, NCL - 1, 1)) - c,
        )

    def plane(body, k):
        for j in range(NRW // CH):
            body(k, j)

    def parts(e, k, extra=False):
        plane(lambda k, j: divide_part(e, k, j, extra), k)

    def spots(j):
        return slice(PAD + CH * j, PAD + CH * (j + 1)), slice(CH * j, CH * (j + 1))

    def step(e, v, body, nxt):
        receive_tiles(e)
        receive_planes(e)
        fix(e, v, 3)
        fix(e, v, 1)
        fix(e, v, 0)
        fix_beyond(e, v)
        plane(body, 3)
        plane(body, 0)
        parts(nxt, 0)
        send_first_plane(nxt)
        send_last_plane(nxt)
        fix(e, v, 2)
        for k in (1, 2):
            plane(body, k)
            parts(nxt, k)
        parts(nxt, 3)
        pack_tiles(nxt)
        send_tiles(nxt)

    for k in range(NPL):
        if k == 0:
            loads[0].wait()
            loads[1].wait()
        parts(pm, k, True)
    pack_tiles(pm)
    pl.semaphore_wait(barrier, sum(jnp.where(here, 1, 0) for here in has))
    send_last_plane(pm)
    send_first_plane(pm)
    send_tiles(pm)
    loads[2].wait()
    for k in range(NPL):
        parts(ps, k, True)
    pack_tiles(ps)
    send_first_plane(ps)
    send_last_plane(ps)
    send_tiles(ps)
    loads[3].wait()
    loads[4].wait()

    def multiply_mid(k, j):
        rows, out = spots(j)
        s = None
        for a in range(3):
            term = cot[a, k, out] * q_all[pm, a, k + 1, rows]
            s = term if s is None else s + term
        inner[k, out] = s

    for k in range(NPL):
        plane(multiply_mid, k)

    def weights(g, w):
        t = g[0] * g[0] + g[1] * g[1] + g[2] * g[2] + DELTA
        rn = lax.rsqrt(t)
        n = t * rn
        r = 1.0 / (w + TAU * n)
        return rn, n, w * r, TAU * r

    def adjoint_mid(k, j):
        rows, out = spots(j)
        g = slopes(v_m, k, j)
        rn, n, h, tr = weights(g, weight[k, out])
        c = [cot[a, k, out] for a in range(3)]
        s = inner[k, out] + TAU * (c[0] * g[0] + c[1] * g[1] + c[2] * g[2])
        m = tr * (h * s)
        f = m * rn
        th = TAU * h
        for a in range(3):
            q_all[cm, a, k + 1, rows] = th * c[a] - f * g[a]
        wacc[k, out] = m * n
        scale[k, out] = h

    step(pm, v_m, adjoint_mid, cm)

    receive_tiles(ps)
    receive_planes(ps)
    for k in range(NPL):
        fix(ps, v_s, k)
    fix_beyond(ps, v_s)

    def prepare_start(k, j):
        rows, out = spots(j)
        for a in range(3):
            hc_o[a, k, out] = scale[k, out] * cot[a, k, out]
        g = slopes(v_s, k, j)
        rn, n, h, tr = weights(g, weight[k, out])
        a1 = tr * h
        aux[0, k, out] = TAU * h
        aux[1, k, out] = a1 * rn
        aux[2, k, out] = a1 * n
        scale[k, out] = h
        for a in range(3):
            gs[a, k, out] = g[a]
            bs[a, k, out] = q_all[ps, a, k + 1, rows] + TAU * g[a]

    for k in range(NPL):
        plane(prepare_start, k)

    def adjoint_start(k, j):
        rows, out = spots(j)
        d = slopes(v_m, k, j)
        c = [hc_o[a, k, out] + d[a] for a in range(3)]
        s = c[0] * bs[0, k, out] + c[1] * bs[1, k, out] + c[2] * bs[2, k, out]
        f = aux[1, k, out] * s
        th = aux[0, k, out]
        for a in range(3):
            q_all[cs, a, k + 1, rows] = th * c[a] - f * gs[a, k, out]
            hc_o[a, k, out] = c[a]
        inner[k, out] = s

    step(cm, v_m, adjoint_start, cs)

    def finish_weight(k, j):
        _, out = spots(j)
        wg_o[k, out] = (wacc[k, out] + aux[2, k, out] * inner[k, out]) / weight[k, out]
        for a in range(3):
            hc_o[a, k, out] = scale[k, out] * hc_o[a, k, out]
        dm_o[k, out] = v_m[k, out]
        u_o[k, out] = u[cs, k, out]

    for k in range(NPL):
        plane(finish_weight, k)
    receive_tiles(cs)
    receive_planes(cs)
    t_o[...] = tbuf[...]
    r_o[...] = rbuf[...]
    fix_beyond(cs, v_s)
    edge_o[1] = v_s[NPL, 0:NRW]
    edge_o[0] = pln[cs, 0]
    for e in range(4):
        tiles_done(e, send_sem)
        pl.when(up_z)(lambda: message(e, 10).wait_send())
        pl.when(low_z)(lambda: message(e, 11).wait_send())


def finish(hc, wg, u, dm, tcol, rrow, edge, dual_h, wg_h, dg_h, v, dual, dg, sem):
    lane = lax.broadcasted_iota(jnp.int32, (CH, NCL), 1)
    row = lax.broadcasted_iota(jnp.int32, (CH, NCL), 0)
    copies = [pltpu.make_async_copy(wg, wg_h, sem.at[0])]
    copies[0].start()
    v[NPL, 0:NRW] = edge[1]
    for k in reversed(range(NPL)):
        for j in range(NRW // CH):
            out = slice(CH * j, CH * (j + 1))
            total = u[k, out] - jnp.where(lane == 0, pltpu.roll(tcol[out], NCL - 2 * k - 1, 1), 0.0)
            if k == 0:
                total = total - edge[0, out]
            if j == 0:
                total = total - jnp.where(row == 0, rrow[2 * k + 1 : 2 * k + 2], 0.0)
            v[k, out] = total
        v[k, NRW : NRW + 1] = rrow[2 * k : 2 * k + 1]
        for j in range(NRW // CH):
            out = slice(CH * j, CH * (j + 1))
            c = v[k, out]
            col = pltpu.roll(tcol[out], NCL - 2 * k - 1, 1)
            dual[0, k, out] = hc[0, k, out] + (v[k + 1, out] - c)
            dual[1, k, out] = hc[1, k, out] + (v[k, CH * j + 1 : CH * (j + 1) + 1] - c)
            dual[2, k, out] = hc[2, k, out] + (jnp.where(lane == NCL - 1, col, pltpu.roll(c, NCL - 1, 1)) - c)
            dg[k, out] = KAPPA * (c + dm[k, out])
        here = [
            pltpu.make_async_copy(dual.at[:, k], dual_h.at[:, k], sem.at[2 * k + 1]),
            pltpu.make_async_copy(dg.at[k], dg_h.at[k], sem.at[2 * k + 2]),
        ]
        for c in here:
            c.start()
        copies += here
    for c in copies:
        c.wait()


def shards(sizes, data, weight, dual_start, dual_mid, cotangent):
    field = (NPL, NRW, NCL)
    vm = pltpu.VMEM
    whole = pl.BlockSpec(memory_space=pltpu.VMEM)
    shapes = (
        jax.ShapeDtypeStruct((3,) + field, F32),
        jax.ShapeDtypeStruct(field, F32),
        jax.ShapeDtypeStruct(field, F32),
    )
    args = (data, weight, dual_start, dual_mid, cotangent)
    face = (NRW, NCL)
    between = ((3,) + field, field, field, field, face, (8, NCL), (2,) + face)
    results = pl.pallas_call(
        functools.partial(kernel, sizes),
        out_shape=[jax.ShapeDtypeStruct(x, F32) for x in between],
        in_specs=[pl.BlockSpec(memory_space=pl.ANY)] * 5,
        out_specs=[whole] * len(between),
        scratch_shapes=[
            vm(field, F32),
            vm(field, F32),
            vm((3,) + field, F32),
            vm((4, 3, NPL + 1, NRW + PAD, NCL), F32),
            vm((4,) + field, F32),
            vm((NPL + 1, NRW + PAD, NCL), F32),
            vm((NPL + 1, NRW + PAD, NCL), F32),
            vm((3,) + field, F32),
            vm((3,) + field, F32),
            vm((3,) + field, F32),
            vm(field, F32),
            vm(field, F32),
            vm(field, F32),
            vm((NRW, NCL), F32),
            vm((NRW, NCL), F32),
            vm(field, F32),
            vm((8, NCL), F32),
            vm((4, 24, NCL), F32),
            vm((4, 10, 8, NCL), F32),
            vm((4, 2, NRW, NCL), F32),
            vm((4, 10, 8, NCL), F32),
            pltpu.SemaphoreType.DMA((5,)),
            pltpu.SemaphoreType.DMA((4, 3)),
            pltpu.SemaphoreType.DMA((4, 3)),
        ],
        compiler_params=pltpu.CompilerParams(
            collective_id=0, has_side_effects=True, vmem_limit_bytes=40 * 1024 * 1024
        ),
    )(*[pltpu.with_memory_space_constraint(x, pltpu.HBM) for x in args])
    return pl.pallas_call(
        finish,
        out_shape=shapes,
        in_specs=[whole] * len(between),
        out_specs=(pl.BlockSpec(memory_space=pl.ANY),) * 3,
        scratch_shapes=[
            vm((NPL + 1, NRW + PAD, NCL), F32),
            vm((3,) + field, F32),
            vm(field, F32),
            pltpu.SemaphoreType.DMA((9,)),
        ],
    )(*[pltpu.with_memory_space_constraint(x, pltpu.VMEM) for x in results])


def solution(mesh):
    field, triple = P("gz", "gx", "gy"), P(None, "gz", "gx", "gy")
    sizes = tuple(mesh.shape[a] for a in AXES)
    return jax.shard_map(
        functools.partial(shards, sizes),
        mesh=mesh,
        in_specs=(field, field, triple, triple, triple),
        out_specs=(triple, field, field),
        check_vma=False,
    )
```

```python
import functools

import jax
import jax.numpy as jnp
from jax import lax
from jax.experimental import pallas as pl
from jax.experimental.pallas import tpu as pltpu
from jax.sharding import PartitionSpec as P

MESH = pl.DeviceIdType.MESH
TAU = 0.08
KAPPA = 0.5
DELTA = 0.01
AXES = ("gx", "gy", "gz")

NPL, NRW, NCL = 4, 128, 128
CH = 32
PAD = 8
R, Z, C = 0, 1, 2
SLOTS = (
    ((-1, 0, 0), R),
    ((1, 0, 0), R),
    ((0, -1, 0), C),
    ((0, 1, 0), C),
    ((-1, 0, 1), R),
    ((1, 0, -1), Z),
    ((0, -1, 1), C),
    ((0, 1, -1), Z),
    ((1, -1, 0), C),
    ((-1, 1, 0), R),
    ((0, 0, -1), None),
    ((0, 0, 1), None),
)
NS = len(SLOTS)
F32 = jnp.float32


def kernel(
    sizes,
    data_h, weight_h, ps_h, pm_h, cot_h,
    hc_o, wg_o, u_o, dm_o, t_o, r_o, edge_o,
    data, weight, cot, q_all, u, v_m, v_s, gs, bs, aux, wacc, scale, inner, xbuf, tbuf, cols, rbuf, tile, rcv, pln, spare,
    in_sem, send_sem, recv_sem,
):
    pos = tuple(lax.axis_index(a) for a in AXES)
    pm, ps, cm, cs = 0, 1, 2, 3
    rest = slice(1, NPL)
    loads = [
        pltpu.make_async_copy(pm_h, q_all.at[pm, :, 1 : NPL + 1, PAD : PAD + NRW], in_sem.at[0]),
        pltpu.make_async_copy(data_h, data, in_sem.at[1]),
    ]
    loads.append(pltpu.make_async_copy(ps_h, q_all.at[ps, :, 1 : NPL + 1, PAD : PAD + NRW], in_sem.at[2]))
    loads.append(pltpu.make_async_copy(weight_h, weight, in_sem.at[3]))
    loads.append(pltpu.make_async_copy(cot_h, cot, in_sem.at[4]))
    for c in loads:
        c.start()

    lane = lax.broadcasted_iota(jnp.int32, (CH, NCL), 1)
    lane8 = lax.broadcasted_iota(jnp.int32, (8, NCL), 1)
    sub8 = lax.broadcasted_iota(jnp.int32, (8, NCL), 0)
    odd = sub8 % 2 == 1

    low_x, low_y, low_z = (p > 0 for p in pos)
    up_x, up_y, up_z = (p < n - 1 for p, n in zip(pos, sizes))

    def exists(off):
        ok = None
        for o, low, up in zip(off, (low_x, low_y, low_z), (up_x, up_y, up_z)):
            if o != 0:
                here = low if o < 0 else up
                ok = here if ok is None else jnp.logical_and(ok, here)
        return ok

    has = [exists(off) for off, _ in SLOTS]
    takes = [exists(tuple(-o for o in off)) for off, _ in SLOTS]
    barrier = pltpu.get_barrier_semaphore()
    for (off, _), here in zip(SLOTS, has):
        @pl.when(here)
        def _():
            peer = tuple(p + o for p, o in zip(pos, off))
            pl.semaphore_signal(barrier, inc=1, device_id=peer, device_id_type=MESH)

    for side, here in ((0, low_z), (1, up_z)):
        @pl.when(jnp.logical_not(here))
        def _():
            for e in range(4):
                pln[e, side] = jnp.zeros((NRW, NCL), F32)

    for e in range(4):
        q_all[e, 0, 0, PAD : PAD + NRW] = jnp.zeros((NRW, NCL), F32)
        for k in range(NPL):
            q_all[e, 1, k + 1, 0:PAD] = jnp.zeros((PAD, NCL), F32)


    def message(e, s):
        off, kind = SLOTS[s]
        if kind is None:
            first = (pm_h.at[0, NPL - 1], ps_h.at[0, NPL - 1], q_all.at[cm, 0, NPL, PAD : PAD + NRW],
                     q_all.at[cs, 0, NPL, PAD : PAD + NRW])
            src = first[e] if s == 10 else u.at[e, 0]
            dst, sem = pln.at[e, s - 10], s - 9
        else:
            src, dst, sem = tile.at[e, 8 * kind : 8 * kind + 8], rcv.at[e, s], 0
        return pltpu.make_async_remote_copy(
            src_ref=src, dst_ref=dst, send_sem=send_sem.at[e, sem], recv_sem=recv_sem.at[e, sem],
            device_id=tuple(p - o for p, o in zip(pos, off)), device_id_type=MESH,
        )

    def filler(e, s, sem):
        kind = SLOTS[s][1]
        dst = rcv.at[e, s] if sem is recv_sem else spare.at[e, s]
        return pltpu.make_async_copy(tile.at[e, 8 * kind : 8 * kind + 8], dst, sem.at[e, 0])

    def tiles_done(e, sem):
        pltpu.make_async_copy(rcv.at[e], rcv.at[e], sem.at[e, 0]).wait()

    def divide_part(e, k, j, extra):
        rows = slice(PAD + CH * j, PAD + CH * (j + 1))
        above = slice(PAD + CH * j - 1, PAD + CH * (j + 1) - 1)
        out = slice(CH * j, CH * (j + 1))
        q2 = q_all[e, 2, k + 1, rows]
        total = q_all[e, 0, k + 1, rows] - q_all[e, 0, k, rows]
        total = total + (q_all[e, 1, k + 1, rows] - q_all[e, 1, k + 1, above])
        total = total + (q2 - jnp.where(lane == 0, 0.0, pltpu.roll(q2, 1, 1)))
        if extra:
            total = total - KAPPA * data[k, out]
        u[e, k, out] = total
        ends = pltpu.roll(jnp.where(lane < NCL // 2, total, q2), 2 * k + 1, 1)
        xbuf[out] = jnp.where(lane // 2 == k, ends, xbuf[out])

    def send_last_plane(e):
        pl.when(up_z)(lambda: message(e, 10).start())

    def send_first_plane(e):
        pl.when(low_z)(lambda: message(e, 11).start())

    def pack_tiles(e):
        for j in range(NRW // CH):
            rows = slice(PAD + CH * j, PAD + CH * (j + 1))
            out = slice(CH * j, CH * (j + 1))
            xbuf[out] = jnp.where(lane == 8, pltpu.roll(q_all[e, 0, NPL, rows], 8, 1), xbuf[out])
        xt = jnp.transpose(xbuf[...])
        tile[e, 16:24] = xt[0:8]
        tile[e, 9:10] = xt[8:9]
        tile[e, 8:9] = q_all[e, 0, NPL, PAD : PAD + 1]
        for k in range(NPL):
            tile[e, 2 * k : 2 * k + 1] = q_all[e, 1, k + 1, PAD + NRW - 1 : PAD + NRW]
            tile[e, 2 * k + 1 : 2 * k + 2] = u[e, k, 0:1]
    def send_tiles(e):
        for s in (6, 7, 8, 9, 2, 3, 4, 5, 0, 1):
            pl.when(takes[s])(lambda: message(e, s).start())
            pl.when(jnp.logical_not(takes[s]))(lambda: filler(e, s, send_sem).start())
            pl.when(jnp.logical_not(has[s]))(lambda: filler(e, s, recv_sem).start())

    def receive_tiles(e):
        tiles_done(e, recv_sem)
        high_c = pltpu.roll(rcv[e, 3], 7, 0) - tile[e, 16:24]
        high_c = high_c - jnp.where(jnp.logical_and(sub8 == 0, low_z), rcv[e, 7, 1:2], 0.0)
        high_c = high_c - jnp.where(jnp.logical_and(lane8 == 0, low_x), rcv[e, 9], 0.0)
        high_c = jnp.where(up_y, high_c, 0.0)
        low_c = jnp.where(low_y, pltpu.roll(rcv[e, 2], 1, 0), 0.0)
        tbuf[0:8] = jnp.where(odd, low_c, high_c)
        tbuf[8:16] = jnp.where(low_y, rcv[e, 6], 0.0)
        tbuf[...] = jnp.transpose(tbuf[...])
        high_r = pltpu.roll(rcv[e, 1], 7, 0) - tile[e, 0:8]
        high_r = high_r - jnp.where(jnp.logical_and(sub8 == 0, low_z), rcv[e, 5, 0:1], 0.0)
        high_r = high_r - jnp.where(jnp.logical_and(lane8 == 0, low_y), rcv[e, 8], 0.0)
        high_r = jnp.where(up_x, high_r, 0.0)
        low_r = jnp.where(low_x, pltpu.roll(rcv[e, 0], 1, 0), 0.0)
        rbuf[...] = jnp.where(odd, low_r, high_r)

    def receive_planes(e):
        pl.when(low_z)(lambda: message(e, 10).wait_recv())
        pl.when(up_z)(lambda: message(e, 11).wait_recv())

    def fix(e, v, k):
        for j in range(NRW // CH):
            out = slice(CH * j, CH * (j + 1))
            col = pltpu.roll(tbuf[out], NCL - 2 * k - 1, 1)
            cols[k, out] = col
            total = u[e, k, out] - jnp.where(lane == 0, col, 0.0)
            if k == 0:
                total = total - pln[e, 0, out]
            v[k, out] = total
        v[k, 0:1] = v[k, 0:1] - rbuf[2 * k + 1 : 2 * k + 2]
        v[k, NRW : NRW + 1] = rbuf[2 * k : 2 * k + 1]

    def fix_beyond(e, v):
        for j in range(NRW // CH):
            rows = slice(PAD + CH * j, PAD + CH * (j + 1))
            out = slice(CH * j, CH * (j + 1))
            col = jnp.where(lane == 0, pltpu.roll(tbuf[out], NCL - 8, 1), 0.0)
            v[NPL, out] = jnp.where(up_z, pln[e, 1, out] - q_all[e, 0, NPL, rows] - col, 0.0)
        v[NPL, 0:1] = v[NPL, 0:1] - jnp.where(jnp.logical_and(up_z, low_x), rcv[e, 4, 0:1], 0.0)

    def slopes(v, k, j):
        out = slice(CH * j, CH * (j + 1))
        c = v[k, out]
        col = cols[k, out]
        return (
            v[k + 1, out] - c,
            v[k, CH * j + 1 : CH * (j + 1) + 1] - c,
            jnp.where(lane == NCL - 1, col, pltpu.roll(c, NCL - 1, 1)) - c,
        )

    def plane(body, k):
        for j in range(NRW // CH):
            body(k, j)

    def parts(e, k, extra=False):
        plane(lambda k, j: divide_part(e, k, j, extra), k)

    def spots(j):
        return slice(PAD + CH * j, PAD + CH * (j + 1)), slice(CH * j, CH * (j + 1))

    def step(e, v, body, nxt):
        receive_tiles(e)
        receive_planes(e)
        fix(e, v, 3)
        fix(e, v, 1)
        fix(e, v, 0)
        fix_beyond(e, v)
        plane(body, 3)
        plane(body, 0)
        parts(nxt, 0)
        send_first_plane(nxt)
        send_last_plane(nxt)
        fix(e, v, 2)
        plane(body, 2)
        parts(nxt, 3)
        plane(body, 1)
        parts(nxt, 2)
        parts(nxt, 1)
        pack_tiles(nxt)
        send_tiles(nxt)

    for k in range(NPL):
        if k == 0:
            loads[0].wait()
            loads[1].wait()
        parts(pm, k, True)
    pack_tiles(pm)
    pl.semaphore_wait(barrier, sum(jnp.where(here, 1, 0) for here in has))
    send_last_plane(pm)
    send_first_plane(pm)
    send_tiles(pm)
    send_last_plane(ps)
    loads[2].wait()
    parts(ps, 0, True)
    send_first_plane(ps)
    for k in range(1, NPL):
        parts(ps, k, True)
    pack_tiles(ps)
    send_tiles(ps)
    loads[3].wait()
    loads[4].wait()

    def multiply_mid(k, j):
        rows, out = spots(j)
        s = None
        for a in range(3):
            term = cot[a, k, out] * q_all[pm, a, k + 1, rows]
            s = term if s is None else s + term
        inner[k, out] = s

    for k in range(NPL):
        plane(multiply_mid, k)

    def weights(g, w):
        t = g[0] * g[0] + g[1] * g[1] + g[2] * g[2] + DELTA
        rn = lax.rsqrt(t)
        n = t * rn
        r = 1.0 / (w + TAU * n)
        return rn, n, w * r, TAU * r

    def adjoint_mid(k, j):
        rows, out = spots(j)
        g = slopes(v_m, k, j)
        rn, n, h, tr = weights(g, weight[k, out])
        c = [cot[a, k, out] for a in range(3)]
        s = inner[k, out] + TAU * (c[0] * g[0] + c[1] * g[1] + c[2] * g[2])
        m = tr * (h * s)
        f = m * rn
        th = TAU * h
        for a in range(3):
            q_all[cm, a, k + 1, rows] = th * c[a] - f * g[a]
        wacc[k, out] = m * n
        scale[k, out] = h

    step(pm, v_m, adjoint_mid, cm)

    receive_tiles(ps)
    receive_planes(ps)
    for k in range(NPL):
        fix(ps, v_s, k)
    fix_beyond(ps, v_s)

    def prepare_start(k, j):
        rows, out = spots(j)
        for a in range(3):
            hc_o[a, k, out] = scale[k, out] * cot[a, k, out]
        g = slopes(v_s, k, j)
        rn, n, h, tr = weights(g, weight[k, out])
        a1 = tr * h
        aux[0, k, out] = TAU * h
        aux[1, k, out] = a1 * rn
        aux[2, k, out] = a1 * n
        scale[k, out] = h
        for a in range(3):
            gs[a, k, out] = g[a]
            bs[a, k, out] = q_all[ps, a, k + 1, rows] + TAU * g[a]

    for k in range(NPL):
        plane(prepare_start, k)

    def adjoint_start(k, j):
        rows, out = spots(j)
        d = slopes(v_m, k, j)
        c = [hc_o[a, k, out] + d[a] for a in range(3)]
        s = c[0] * bs[0, k, out] + c[1] * bs[1, k, out] + c[2] * bs[2, k, out]
        f = aux[1, k, out] * s
        th = aux[0, k, out]
        for a in range(3):
            q_all[cs, a, k + 1, rows] = th * c[a] - f * gs[a, k, out]
            hc_o[a, k, out] = c[a]
        inner[k, out] = s

    step(cm, v_m, adjoint_start, cs)

    def finish_weight(k, j):
        _, out = spots(j)
        wg_o[k, out] = (wacc[k, out] + aux[2, k, out] * inner[k, out]) / weight[k, out]
        for a in range(3):
            hc_o[a, k, out] = scale[k, out] * hc_o[a, k, out]
        dm_o[k, out] = v_m[k, out]
        u_o[k, out] = u[cs, k, out]

    for k in range(NPL):
        plane(finish_weight, k)
    receive_tiles(cs)
    receive_planes(cs)
    t_o[...] = tbuf[...]
    r_o[...] = rbuf[...]
    fix_beyond(cs, v_s)
    edge_o[1] = v_s[NPL, 0:NRW]
    edge_o[0] = pln[cs, 0]
    for e in range(4):
        tiles_done(e, send_sem)
        pl.when(up_z)(lambda: message(e, 10).wait_send())
        pl.when(low_z)(lambda: message(e, 11).wait_send())


def finish(hc, wg, u, dm, tcol, rrow, edge, dual_h, wg_h, dg_h, v, dual, dg, sem):
    lane = lax.broadcasted_iota(jnp.int32, (CH, NCL), 1)
    copies = [pltpu.make_async_copy(wg, wg_h, sem.at[0])]
    copies[0].start()
    v[NPL, 0:NRW] = edge[1]
    for k in reversed(range(NPL)):
        for j in range(NRW // CH):
            out = slice(CH * j, CH * (j + 1))
            total = u[k, out] - jnp.where(lane == 0, pltpu.roll(tcol[out], NCL - 2 * k - 1, 1), 0.0)
            if k == 0:
                total = total - edge[0, out]
            v[k, out] = total
        v[k, 0:1] = v[k, 0:1] - rrow[2 * k + 1 : 2 * k + 2]
        v[k, NRW : NRW + 1] = rrow[2 * k : 2 * k + 1]
        for j in range(NRW // CH):
            out = slice(CH * j, CH * (j + 1))
            c = v[k, out]
            col = pltpu.roll(tcol[out], NCL - 2 * k - 1, 1)
            dual[0, k, out] = hc[0, k, out] + (v[k + 1, out] - c)
            dual[1, k, out] = hc[1, k, out] + (v[k, CH * j + 1 : CH * (j + 1) + 1] - c)
            dual[2, k, out] = hc[2, k, out] + (jnp.where(lane == NCL - 1, col, pltpu.roll(c, NCL - 1, 1)) - c)
            dg[k, out] = KAPPA * (c + dm[k, out])
        here = [
            pltpu.make_async_copy(dual.at[:, k], dual_h.at[:, k], sem.at[2 * k + 1]),
            pltpu.make_async_copy(dg.at[k], dg_h.at[k], sem.at[2 * k + 2]),
        ]
        for c in here:
            c.start()
        copies += here
    for c in copies:
        c.wait()


def shards(sizes, data, weight, dual_start, dual_mid, cotangent):
    field = (NPL, NRW, NCL)
    vm = pltpu.VMEM
    whole = pl.BlockSpec(memory_space=pltpu.VMEM)
    shapes = (
        jax.ShapeDtypeStruct((3,) + field, F32),
        jax.ShapeDtypeStruct(field, F32),
        jax.ShapeDtypeStruct(field, F32),
    )
    args = (data, weight, dual_start, dual_mid, cotangent)
    face = (NRW, NCL)
    between = ((3,) + field, field, field, field, face, (8, NCL), (2,) + face)
    results = pl.pallas_call(
        functools.partial(kernel, sizes),
        out_shape=[jax.ShapeDtypeStruct(x, F32) for x in between],
        in_specs=[pl.BlockSpec(memory_space=pl.ANY)] * 5,
        out_specs=[whole] * len(between),
        scratch_shapes=[
            vm(field, F32),
            vm(field, F32),
            vm((3,) + field, F32),
            vm((4, 3, NPL + 1, NRW + PAD, NCL), F32),
            vm((4,) + field, F32),
            vm((NPL + 1, NRW + PAD, NCL), F32),
            vm((NPL + 1, NRW + PAD, NCL), F32),
            vm((3,) + field, F32),
            vm((3,) + field, F32),
            vm((3,) + field, F32),
            vm(field, F32),
            vm(field, F32),
            vm(field, F32),
            vm((NRW, NCL), F32),
            vm((NRW, NCL), F32),
            vm(field, F32),
            vm((8, NCL), F32),
            vm((4, 24, NCL), F32),
            vm((4, 10, 8, NCL), F32),
            vm((4, 2, NRW, NCL), F32),
            vm((4, 10, 8, NCL), F32),
            pltpu.SemaphoreType.DMA((5,)),
            pltpu.SemaphoreType.DMA((4, 3)),
            pltpu.SemaphoreType.DMA((4, 3)),
        ],
        compiler_params=pltpu.CompilerParams(
            collective_id=0, has_side_effects=True, vmem_limit_bytes=40 * 1024 * 1024
        ),
    )(*[pltpu.with_memory_space_constraint(x, pltpu.HBM) for x in args])
    return pl.pallas_call(
        finish,
        out_shape=shapes,
        in_specs=[whole] * len(between),
        out_specs=(pl.BlockSpec(memory_space=pl.ANY),) * 3,
        scratch_shapes=[
            vm((NPL + 1, NRW + PAD, NCL), F32),
            vm((3,) + field, F32),
            vm(field, F32),
            pltpu.SemaphoreType.DMA((9,)),
        ],
    )(*[pltpu.with_memory_space_constraint(x, pltpu.VMEM) for x in results])


def solution(mesh):
    field, triple = P("gz", "gx", "gy"), P(None, "gz", "gx", "gy")
    sizes = tuple(mesh.shape[a] for a in AXES)
    return jax.shard_map(
        functools.partial(shards, sizes),
        mesh=mesh,
        in_specs=(field, field, triple, triple, triple),
        out_specs=(triple, field, field),
        check_vma=False,
    )
```
